256 devices in a mesh: dp: 8 (over y, core), seq: 32 (over x, z).
Axes of the slice: x: 4, y: 4, z: 8, core: 2. Of those that a mesh axis runs over, the one named last changes fastest.
Arguments:
- inputs: bfloat16 [8, 4096, 4096], P('dp', 'seq'), may hold values from -6 to 6
- gates: bfloat16 [8, 4096, 4096], P('dp', 'seq'), may hold values from -6 to 6
- keys_b: bfloat16 [8, 4096, 128], P('dp', 'seq'), may hold values from -2 to 2
- reads_c: bfloat16 [8, 4096, 128], P('dp', 'seq'), may hold values from -2 to 2
- step_codes: int32 [8, 4096], P('dp', 'seq'), may hold values from 1 to 16
- seg_starts: int32 [8, 4096], P('dp', 'seq'), may hold values 0 or 1
- targets: bfloat16 [8, 4096, 4096], P('dp', 'seq'), may hold values from -6 to 6
- log_rates: float32 [64], replicated
- skips: float32 [64], replicated, may hold values from 0.5 to 2
- gains: float32 [4096], replicated, may hold values from 0.5 to 1.5
Outputs:
- loss: float32 [], replicated
- grad_inputs: bfloat16 [8, 4096, 4096], P('dp', 'seq')
- grad_gates: bfloat16 [8, 4096, 4096], P('dp', 'seq')
- grad_keys: bfloat16 [8, 4096, 128], P('dp', 'seq')
- grad_reads: bfloat16 [8, 4096, 128], P('dp', 'seq')
- grad_rates: float32 [64], replicated
- grad_skips: float32 [64], replicated
- grad_gains: float32 [4096], replicated
The draws below stay inside these ranges and needn't reach their ends.
All inputs are finite; a program needn't handle non-finite values. No bound on the sum of `seg_starts` on one device may be relied on, other than what follows from the above.
Results may differ from the reference program's by a relative error of at most 0.012.
Values sent between devices are 32-bit elements; how exact they have to be, the bound alone decides.
A program may use at most 192 MiB of HBM per device.

```python
import math
import jax
import jax.numpy as jnp
from jax import lax

HEADS = 64
N = 128
TOK_DEV = 128
W = 4096
TOKENS = 4096
TRACES = 8


def draw_log_rates(key, part):
    key_pick = jax.random.fold_in(key, 11)
    key_slow = jax.random.fold_in(key, 12)
    key_fast = jax.random.fold_in(key, 13)
    share = 0.5
    is_slow = jax.random.uniform(key_pick, (HEADS,)) < share
    slow_vals = jax.random.uniform(key_slow, (HEADS,), minval=math.log(0.1), maxval=math.log(1.5)) - math.log(TOKENS * 0.133)
    fast_vals = jax.random.uniform(key_fast, (HEADS,), minval=-2.1, maxval=-0.9)
    return jnp.where(is_slow, slow_vals, fast_vals).astype(jnp.float32)


def with_ends(drawn, key, least, top_value):
    dims = drawn.shape
    index_at = [jax.random.randint(jax.random.fold_in(key, axis), (), 0, dims[axis]) for axis in range(len(dims))]
    drawn = drawn.at[tuple(index_at)].set(least)
    longest = dims.index(max(dims))
    index_at[longest] = (index_at[longest] + 1) % dims[longest]
    return drawn.at[tuple(index_at)].set(top_value)


def block_scale(own_key, extent, cuts, smallest, high):
    def one(position, parts):
        steps = jax.random.uniform(jax.random.fold_in(jax.random.fold_in(own_key, 6), position), (parts,), jnp.float32, smallest / len(cuts), high / len(cuts))
        return jnp.repeat(jnp.exp(steps), extent[position] // parts).reshape((-1,) + (1,) * (len(extent) - position - 1))

    factor_of = one(*cuts[0])
    for cut in cuts[1:]:
        factor_of = factor_of * one(*cut)
    return factor_of


def bell_draw(own_key, shape, scale, bound, shards=(), held_as=jnp.bfloat16):
    loudness = block_scale(own_key, shape, shards, -0.22, 0.18) if shards else 1.0
    drawn = jax.random.normal(own_key, shape, jnp.float32) * scale * loudness
    return jnp.minimum(jnp.maximum(drawn, -bound), bound).astype(held_as)


def setup_inputs(seed: int = 0) -> dict:
    arg_keys = jax.random.split(jax.random.key(seed), 11)
    inputs = bell_draw(arg_keys[0], (TRACES, TOKENS, W), 1.0, 6.0, ((0, 8), (1, 32)))
    gates = bell_draw(arg_keys[1], (TRACES, TOKENS, W), 1.0, 6.0, ((0, 8), (1, 32)))
    keys_b = bell_draw(arg_keys[2], (TRACES, TOKENS, N), 0.3, 2.0, ((0, 8), (1, 32)))
    reads_c = bell_draw(arg_keys[3], (TRACES, TOKENS, N), 0.3, 2.0, ((0, 8), (1, 32)))
    step_codes = with_ends(jax.random.randint(arg_keys[4], (TRACES, TOKENS), 1, 17), jax.random.fold_in(arg_keys[4], 1), 1, 16).astype(jnp.int32)
    seg_starts = with_ends((jax.random.randint(arg_keys[5], (TRACES, TOKENS), 0, TOK_DEV * 8) < 1).astype(jnp.int32), jax.random.fold_in(arg_keys[5], 1), 0, 1)
    targets = bell_draw(arg_keys[6], (TRACES, TOKENS, W), 1.0, 6.0, ((0, 8), (1, 32)))
    log_rates = draw_log_rates(jax.random.fold_in(arg_keys[10], 71), 0)
    skips = jnp.clip(jax.random.uniform(arg_keys[8], (HEADS,), jnp.float32, 0.5, 2.0), 0.5, 2.0)
    gains = jnp.clip(1.0 + 0.1 * jax.random.normal(arg_keys[9], (W,), jnp.float32), 0.5, 1.5)
    return dict(inputs=inputs, gates=gates, keys_b=keys_b, reads_c=reads_c, step_codes=step_codes, seg_starts=seg_starts, targets=targets, log_rates=log_rates, skips=skips, gains=gains)


def decays(step_codes, seg_starts, log_rates):
    timestep = step_codes.astype(jnp.float32) / 64.0
    rate_vals = jnp.exp(log_rates)
    cumulative = jnp.cumsum(-timestep[:, None] * rate_vals[None, :], axis=0)
    segment = jnp.cumsum(seg_starts, axis=0, dtype=jnp.int32)
    return (timestep, cumulative, segment)

def local_state(inputs, keys_b, step_codes, seg_starts, log_rates):
    timestep, cumulative, segment = decays(step_codes, seg_starts, log_rates)
    length = inputs.shape[0]
    n_heads = log_rates.shape[0]
    keep_end = (segment == segment[-1]).astype(jnp.float32)
    weight = jnp.exp(cumulative[-1][None, :] - cumulative) * keep_end[:, None] * timestep[:, None]
    scaled = (inputs.reshape(length, n_heads, -1).astype(jnp.float32) * weight[:, :, None]).astype(jnp.bfloat16)
    state_sum = jnp.einsum('shp,sn->hpn', scaled.astype(jnp.float32), keys_b.astype(jnp.float32), precision=lax.Precision.HIGHEST)
    unbroken = (segment[-1] == 0).astype(jnp.float32)
    growth = unbroken * jnp.exp(cumulative[-1])
    return (state_sum, growth)

def intra_block(inner_cb, visible, timestep, cum_group, x_group):
    spread_log = cum_group.T[:, :, None] - cum_group.T[:, None, :]
    decay_tab = jnp.where(visible[None], jnp.exp(jnp.where(visible[None], spread_log, 0.0)), 0.0)
    scores = (inner_cb[None] * decay_tab * timestep[None, None, :]).astype(jnp.bfloat16)
    return jnp.einsum('hts,shp->thp', scores.astype(jnp.float32), x_group.astype(jnp.float32), precision=lax.Precision.HIGHEST)

def local_output(inputs, gates, keys_b, reads_c, step_codes, seg_starts, targets, log_rates, skips, gains, incoming):
    timestep, cumulative, segment = decays(step_codes, seg_starts, log_rates)
    length = inputs.shape[0]
    n_heads = log_rates.shape[0]
    inner_width = inputs.shape[1]
    head_size = inner_width // n_heads
    carried = (segment == 0).astype(jnp.float32)[:, None] * jnp.exp(cumulative)
    inner_cb = jnp.dot(reads_c, keys_b.T, preferred_element_type=jnp.float32)
    positions = jnp.arange(length)
    visible = (positions[:, None] >= positions[None, :]) & (segment[:, None] == segment[None, :])
    x_heads = inputs.reshape(length, n_heads, head_size)
    block_heads = math.gcd(n_heads, 8)
    pieces = []
    for offset in range(0, n_heads, block_heads):
        pieces.append(jax.checkpoint(intra_block)(inner_cb, visible, timestep, cumulative[:, offset:offset + block_heads], x_heads[:, offset:offset + block_heads]))
    inside = jnp.concatenate(pieces, axis=1)
    entering = carried[:, :, None] * jnp.einsum('tn,hpn->thp', reads_c.astype(jnp.float32), incoming, precision=lax.Precision.HIGHEST)
    mixture = inside + entering + skips[None, :, None] * x_heads.astype(jnp.float32)
    gated_vals = mixture.reshape(length, inner_width) * jax.nn.silu(gates.astype(jnp.float32))
    normed = gated_vals * lax.rsqrt(lax.optimization_barrier(jnp.mean(gated_vals * gated_vals, axis=-1, keepdims=True)) + 1e-05) * gains
    mismatch = normed - targets.astype(jnp.float32)
    return 0.5 * jnp.sum(mismatch * mismatch)

def reference(inputs, gates, keys_b, reads_c, step_codes, seg_starts, targets, log_rates, skips, gains):

    def trace_loss(pack, rate_logs, skip_vals, gain_vals):
        n_blocks = pack[0].shape[0] // TOK_DEV

        def reshape_blocks(array):
            return array.reshape((n_blocks, TOK_DEV) + array.shape[1:])
        packs = tuple((reshape_blocks(array) for array in pack))
        n_heads = rate_logs.shape[0]
        head_size = pack[0].shape[1] // n_heads

        def block_step(state_sum, blocks):
            x_blk, z_blk, b_blk, c_blk, k_blk, s_blk, t_blk = blocks
            loss_here = local_output(x_blk, z_blk, b_blk, c_blk, k_blk, s_blk, t_blk, rate_logs, skip_vals, gain_vals, state_sum)
            block_state, growth = local_state(x_blk, b_blk, k_blk, s_blk, rate_logs)
            return (growth[:, None, None] * state_sum + block_state, loss_here)
        start_state = jnp.zeros((n_heads, head_size, pack[2].shape[1]), jnp.float32)
        _, losses = lax.scan(jax.checkpoint(block_step), start_state, packs)
        return jnp.sum(losses)

    def summed_loss(x_all, z_all, b_all, c_all, rate_logs, skip_vals, gain_vals):

        def per_trace(pack):
            return trace_loss(pack, rate_logs, skip_vals, gain_vals)
        losses = lax.map(per_trace, (x_all, z_all, b_all, c_all, step_codes, seg_starts, targets))
        return jnp.sum(losses)
    summed, pullback = jax.vjp(summed_loss, inputs, gates, keys_b, reads_c, log_rates, skips, gains)
    grad_x, grad_z, grad_b, grad_c, grad_rate, grad_skip, grad_gain = pullback(jnp.float32(1.0))
    row_count = jnp.float32(inputs.shape[0] * inputs.shape[1])
    return (summed / row_count, grad_x, grad_z, grad_b, grad_c, grad_rate / row_count, grad_skip / row_count, grad_gain / row_count)
```

```python
import functools

import jax
import jax.numpy as jnp
from jax import lax
from jax.experimental import pallas as pl
from jax.experimental.pallas import tpu as pltpu
from jax.sharding import PartitionSpec as P

F32, BF16 = jnp.float32, jnp.bfloat16
LANES = 128
Z_RING = 8
SPLIT = 2
LAG = (9, 8)


def red8(v):
    return v.reshape(v.shape[0] // 8, 8, LANES).sum(axis=0)


def mm(a, b):
    return lax.dot_general(a, b, (((1,), (0,)), ((), ())), preferred_element_type=F32)


def mm_nt(a, b):
    return lax.dot_general(a, b, (((1,), (1,)), ((), ())), preferred_element_type=F32)


def mm_tn(a, b):
    return lax.dot_general(a, b, (((0,), (0,)), ((), ())), preferred_element_type=F32)


def kernel(
    xr, zr, dpn, nb, rows_total,
    lr, sk, x, z, tg, bk, ck, codes, segs, gains,
    gx, gz, gb, gc, red,
    s_st, p_st, k_st, d_st, r_st, q_st,
    mix, ebuf, dxa, inter, ub,
    cols, tab, acc, ga, sa, ra, bt, ct, meta, arz, arx, ard,
    f_recv, f_carry, b_recv, b_carry, sends, msems,
    z_ss, z_rs, x_ss, x_rs, d_ss, d_rs,
):
    tok = x.shape[0]
    width = nb * LANES
    me, dpi = lax.axis_index("seq"), lax.axis_index("dp")
    zi, xi = lax.rem(me, zr), lax.div(me, zr)
    z_at = lambda k: {"seq": xi * zr + lax.rem(zi + k, zr)}
    x_at = lambda k: {"seq": lax.rem(xi + k, xr) * zr + zi}
    d_at = lambda k: {"dp": lax.rem(dpi + k, dpn)}

    barrier = pltpu.get_barrier_semaphore()
    peers = [z_at(k) for k in range(1, zr)] + [x_at(k) for k in range(1, xr)] + [d_at(k) for k in range(1, dpn)]
    for peer in peers:
        pl.semaphore_signal(barrier, inc=1, device_id=peer, device_id_type=pl.DeviceIdType.MESH)

    t_i = lax.broadcasted_iota(jnp.int32, (tok, tok), 0)
    s_i = lax.broadcasted_iota(jnp.int32, (tok, tok), 1)
    diag, upto = t_i == s_i, s_i <= t_i

    def forms(row):
        wide = jnp.broadcast_to(row, (tok, tok))
        own = jnp.sum(jnp.where(diag, wide, 0.0), axis=1, keepdims=True)
        col = jnp.sum(jnp.where(upto, wide, 0.0), axis=1, keepdims=True)
        across = jnp.sum(jnp.where(t_i <= s_i, jnp.broadcast_to(own, (tok, tok)), 0.0), axis=0, keepdims=True)
        return own, col, across, jnp.sum(row, axis=1, keepdims=True)

    code_row = codes[...].astype(F32)
    code_own, cum_col, cum_row, cum_end = forms(code_row)
    _, seg_col, seg_row, seg_end = forms(segs[...].astype(F32))
    visible = upto & (seg_col == seg_row)
    c_mat, b_mat = ck[...], bk[...]
    dt_row = code_row * (1.0 / 64.0)
    gap = jnp.where(visible, (cum_col - cum_row) * (1.0 / 64.0), 0.0)
    dt_vis = jnp.where(visible, jnp.broadcast_to(dt_row, (tok, tok)), 0.0)
    cb_dt = mm_nt(c_mat, b_mat) * dt_vis
    tab[0], tab[1], tab[2], tab[3] = gap, cb_dt, cb_dt * gap, dt_vis
    shape = (tok, LANES)
    cols[0] = jnp.broadcast_to(cum_col * (1.0 / 64.0), shape)
    cols[1] = jnp.broadcast_to((cum_end - cum_col) * (1.0 / 64.0), shape)
    cols[2] = jnp.broadcast_to(jnp.where(seg_col == seg_end, code_own * (1.0 / 64.0), 0.0), shape)
    cols[3] = jnp.broadcast_to((seg_col == 0.0).astype(F32), shape)
    bt[...], ct[...] = b_mat.astype(F32).T.astype(BF16), c_mat.astype(F32).T.astype(BF16)
    end_dt = jnp.broadcast_to(cum_end * (1.0 / 64.0), (1, LANES))
    broken = jnp.broadcast_to((seg_end > 0.0).astype(F32), (1, LANES))
    meta[6] = jnp.where(
        lax.broadcasted_iota(jnp.int32, (8, LANES), 0) == 0, end_dt,
        jnp.where(lax.broadcasted_iota(jnp.int32, (8, LANES), 0) == 1, broken, 0.0),
    )
    acc[...] = jnp.zeros_like(acc)

    low = lax.broadcasted_iota(jnp.int32, (1, LANES), 1) < LANES // 2

    def rates(b):
        a0 = jnp.exp(jnp.full((1, LANES), lr[2 * b], F32))
        a1 = jnp.exp(jnp.full((1, LANES), lr[2 * b + 1], F32))
        return a0, a1, jnp.where(low, a0, a1)

    def skip_row(b):
        return jnp.where(low, jnp.full((1, LANES), sk[2 * b], F32), jnp.full((1, LANES), sk[2 * b + 1], F32))

    def decay_of(m, a):
        return jnp.where(m[1:2] > 0.0, 0.0, jnp.exp(-a * m[0:1]))

    def lanes(b):
        return pl.ds(pl.multiple_of(b * LANES, LANES), LANES)

    def pair(b):
        xb = x[:, lanes(b)]
        zero = jnp.zeros_like(xb)
        return jnp.concatenate([jnp.where(low, xb, zero), jnp.where(low, zero, xb)], axis=0)

    part = tok // SPLIT

    class Pass:
        def __init__(self, pos, row, up, down, across, out, recv, carry, recv_sem, carry_sem, sem0):
            self.pos, self.row, self.up, self.down, self.across = pos, row, up, down, across
            self.out, self.recv, self.carry = out, recv, carry
            self.recv_sem, self.carry_sem, self.sem0 = recv_sem, carry_sem, sem0
            self.lag = jnp.where(row == 0, 0, lax.div((2 * (zr - 1) + row - 2 * pos) * LAG[0], LAG[1]))

        def copy(self, src, dst, b, q, send, recv, to):
            cut = (b, pl.ds(q * part, part))
            return pltpu.make_async_remote_copy(
                src_ref=src.at[cut], dst_ref=dst.at[cut], send_sem=sends.at[self.sem0 + send],
                recv_sem=recv.at[b * SPLIT + q], device_id=to, device_id_type=pl.DeviceIdType.MESH,
            )

        def head(self):
            m = self.sem0
            move = pltpu.make_async_remote_copy(
                src_ref=meta.at[m + 1], dst_ref=meta.at[m], send_sem=msems.at[m], recv_sem=msems.at[m + 1],
                device_id=self.up, device_id_type=pl.DeviceIdType.MESH,
            )

            @pl.when(self.pos == 0)
            def _():
                meta[m] = jnp.zeros((8, LANES), F32)

            @pl.when(self.pos > 0)
            def _():
                move.wait_recv()

            meta[m + 1] = meta[m] + meta[6]

            @pl.when(self.pos < zr - 1)
            def _():
                move.start()

            return move

        def scan(self, b):
            _, _, a = rates(b)
            g = decay_of(meta[6], a)
            for q in range(SPLIT):
                cut = (b, pl.ds(q * part, part))
                move = self.copy(self.out, self.recv, b, q, 0, self.recv_sem, self.up)

                @pl.when(self.pos > 0)
                def _():
                    move.wait_recv()
                    self.out[cut] = self.out[cut] + g * self.recv[cut]

                @pl.when(self.pos == 0)
                def _():
                    self.recv[cut] = jnp.zeros((part, LANES), F32)

                @pl.when(self.pos < zr - 1)
                def _():
                    move.start()

        def take(self, b):
            _, _, a = rates(b)
            for q in range(SPLIT):
                cut = (b, pl.ds(q * part, part))
                onward = self.copy(self.carry, self.carry, b, q, 1, self.carry_sem, self.down)

                @pl.when(self.row > 0)
                def _():
                    onward.wait_recv()

                    @pl.when(self.pos > 0)
                    def _():
                        onward.start()

                @pl.when((self.pos == zr - 1) & (self.row < xr - 1))
                def _():
                    @pl.when(self.row > 0)
                    def _():
                        self.out[cut] = self.out[cut] + decay_of(meta[self.sem0 + 1], a) * self.carry[cut]

                    self.copy(self.out, self.carry, b, q, 0, self.carry_sem, self.across).start()

                @pl.when(self.row > 0)
                def _():
                    self.recv[cut] = self.recv[cut] + decay_of(meta[self.sem0], a) * self.carry[cut]

        def finish(self, move):
            @pl.when(self.pos < zr - 1)
            def _():
                move.wait_send()

            whole = lambda src, send, recv: pltpu.make_async_remote_copy(
                src_ref=src, dst_ref=src, send_sem=sends.at[self.sem0 + send], recv_sem=recv.at[0],
                device_id=self.up, device_id_type=pl.DeviceIdType.MESH,
            )

            @pl.when((self.pos < zr - 1) | (self.row < xr - 1))
            def _():
                whole(self.out, 0, self.recv_sem).wait_send()

            @pl.when((self.row > 0) & (self.pos > 0))
            def _():
                whole(self.carry, 1, self.carry_sem).wait_send()

        def run(self, make, beside, then):
            def step(i, carry):
                @pl.when(i < nb)
                def _():
                    make(i)
                    self.scan(i)
                    beside(i)

                @pl.when(i >= self.lag)
                def _():
                    self.take(i - self.lag)
                    then(i - self.lag)

                return carry

            lax.fori_loop(0, nb + self.lag, step, 0)

    fwd = Pass(zi, xi, z_at(1), z_at(zr - 1), x_at(1), s_st, p_st, k_st, f_recv, f_carry, 0)
    bwd = Pass(zr - 1 - zi, xr - 1 - xi, z_at(zr - 1), z_at(1), x_at(xr - 1), d_st, r_st, q_st, b_recv, b_carry, 2)

    def block_state(b):
        _, _, a = rates(b)
        u = (x[:, lanes(b)].astype(F32) * (jnp.exp(-a * cols[1]) * cols[2])).astype(BF16)
        ub[:, lanes(b)] = u
        s_st[b] = mm(bt[...], u)

    def scores_of(b):
        a0, a1, _ = rates(b)
        gap, cbd = tab[0], tab[1]
        e0, e1 = jnp.exp(-a0 * gap), jnp.exp(-a1 * gap)
        both = jnp.concatenate([(cbd * e0).astype(BF16), (cbd * e1).astype(BF16)], axis=1)
        return e0, e1, both

    def inside(b):
        _, _, both = scores_of(b)
        mix[:, lanes(b)] = mm(both, pair(b)) + skip_row(b) * x[:, lanes(b)].astype(F32)

    def mixture(b):
        _, _, a = rates(b)
        at = lanes(b)
        state = p_st[b].astype(BF16)
        inter[b] = state
        e = mm(c_mat_ref[...], state)
        ebuf[:, at] = e
        m = mix[:, at] + jnp.exp(-a * cols[0]) * cols[3] * e
        mix[:, at] = m
        zf = z[:, at].astype(F32)
        gated = m * (zf / (1.0 + jnp.exp(-zf)))
        gg = gated * gains[:, at]
        acc[0] += gated * gated
        acc[1] += gg * gg
        acc[2] += gg * tg[:, at].astype(F32)

    c_mat_ref, b_mat_ref = ck, bk

    pl.semaphore_wait(barrier, len(peers))
    first = fwd.head()
    fwd.run(block_state, inside, mixture)

    squares = jnp.sum(acc[0], axis=1, keepdims=True)
    r_col = lax.rsqrt(squares * (1.0 / width) + 1e-5)
    coef = r_col * r_col * r_col * (1.0 / width) * (
        r_col * jnp.sum(acc[1], axis=1, keepdims=True) - jnp.sum(acc[2], axis=1, keepdims=True)
    )
    cols[4] = jnp.broadcast_to(r_col, shape)
    cols[5] = jnp.broadcast_to(coef, shape)

    def direct(b):
        _, _, a = rates(b)
        at = lanes(b)
        m, xf, zf, gain, r = mix[:, at], x[:, at].astype(F32), z[:, at].astype(F32), gains[:, at], cols[4]
        sig = 1.0 / (1.0 + jnp.exp(-zf))
        sg = zf * sig
        gated = m * sg
        unit = gated * r
        miss = unit * gain - tg[:, at].astype(F32)
        dgated = r * (miss * gain) - gated * cols[5]
        dmix = dgated * sg
        de = jnp.exp(-a * cols[0]) * cols[3] * dmix
        deb = de.astype(BF16)
        d_st[b] = mm(ct[...], deb)
        mix[:, at] = dmix
        gz[:, at] = (dgated * m * (sig * (1.0 + zf * (1.0 - sig)))).astype(BF16)
        acc[3, 0:8] += red8(miss * miss)
        ga[b] = red8(miss * unit)
        sa[b] = red8(dmix * xf)
        ra[b] = red8(cols[0] * de * ebuf[:, at])
        acc[4] += mm_nt(deb, inter[b])

    def inside_back(b):
        at = lanes(b)
        e0, e1, both = scores_of(b)
        dmix = mix[:, at]
        dmb = dmix.astype(BF16)
        ds = mm_nt(dmb, pair(b))
        d0, d1 = ds[:, :tok] * e0, ds[:, tok:] * e1
        acc[5] += d0 + d1
        v0, v1 = red8(d0 * tab[2]), red8(d1 * tab[2])
        ra[b] += jnp.where(low, v0 + pltpu.roll(v0, LANES // 2, 1), v1 + pltpu.roll(v1, LANES // 2, 1))
        back = mm_tn(both, dmb)
        dxa[:, at] = jnp.where(low, back[:tok], back[tok:]) + skip_row(b) * dmix

    def state_back(b):
        _, _, a = rates(b)
        at = lanes(b)
        by = r_st[b]
        byb = by.astype(BF16)
        duw = mm(b_mat_ref[...], byb) * (jnp.exp(-a * cols[1]) * cols[2])
        gx[:, at] = (dxa[:, at] + duw).astype(BF16)
        own = meta[6]
        ra[b] += red8(cols[1] * duw * x[:, at].astype(F32)) + red8(by * p_st[b]) * (own[0:1] * decay_of(own, a))
        acc[6] += mm_nt(ub[:, at], byb)

    second = bwd.head()
    bwd.run(direct, inside_back, state_back)

    dcb = (acc[5] * tab[3]).astype(BF16)
    gc[...] = (acc[4] + mm(dcb, bk[...])).astype(BF16)
    gb[...] = (acc[6] + mm_tn(dcb, ck[...])).astype(BF16)

    lane8 = lax.broadcasted_iota(jnp.int32, (8, LANES), 1)
    a_rows = jnp.concatenate([rates(b)[2] for b in range(nb)], axis=0)
    halves = lambda rows: (
        jnp.sum(jnp.where(low, rows, 0.0), axis=1, keepdims=True),
        jnp.sum(jnp.where(low, 0.0, rows), axis=1, keepdims=True),
    )
    packed = jnp.where(lane8 == 127, jnp.broadcast_to(0.5 * jnp.sum(acc[3, 0:8], axis=1, keepdims=True), (8, LANES)), 0.0)
    for base, rows in ((0, ra[...].sum(axis=1) * -a_rows), (64, sa[...].sum(axis=1))):
        h0, h1 = halves(rows)
        for g in range(nb // 8):
            cut = slice(8 * g, 8 * g + 8)
            packed += jnp.where(lane8 == base + 2 * g, h0[cut], 0.0) + jnp.where(lane8 == base + 2 * g + 1, h1[cut], 0.0)
    total = jnp.concatenate([ga[...].sum(axis=1), packed], axis=0)

    for buf, mine, n, at, ss, rs in ((arz, zi, zr, z_at, z_ss, z_rs), (arx, xi, xr, x_at, x_ss, x_rs), (ard, dpi, dpn, d_at, d_ss, d_rs)):
        buf[mine] = total

        def hop(k, slot):
            return pltpu.make_async_remote_copy(
                src_ref=buf.at[slot], dst_ref=buf.at[slot], send_sem=ss.at[k], recv_sem=rs.at[k],
                device_id=at(k), device_id_type=pl.DeviceIdType.MESH,
            )

        for k in range(1, n):
            hop(k, mine).start()
        for k in range(1, n):
            hop(k, lax.rem(mine + n - k, n)).wait_recv()
        total = buf[0]
        for k in range(1, n):
            total = total + buf[k]
        for k in range(1, n):
            hop(k, mine).wait_send()
    red[...] = total * (1.0 / rows_total)
    fwd.finish(first)
    bwd.finish(second)


def shards(mesh, inputs, gates, keys_b, reads_c, step_codes, seg_starts, targets, log_rates, skips, gains):
    tok, width = inputs.shape[1:]
    nb = width // LANES
    seq, dpn = mesh.shape["seq"], mesh.shape["dp"]
    zr = min(Z_RING, seq)
    xr = seq // zr
    vmem, smem = pl.BlockSpec(memory_space=pltpu.VMEM), pl.BlockSpec(memory_space=pltpu.SMEM)
    rows = nb + 8
    state = pltpu.VMEM((nb, tok, LANES), F32)
    dma = pltpu.SemaphoreType.DMA
    wide = jax.ShapeDtypeStruct((tok, width), BF16)
    small = jax.ShapeDtypeStruct(keys_b.shape[1:], BF16)
    gx, gz, gb, gc, red = pl.pallas_call(
        functools.partial(kernel, xr, zr, dpn, nb, float(tok * seq * dpn)),
        out_shape=(wide, wide, small, small, jax.ShapeDtypeStruct((rows, LANES), F32)),
        in_specs=[smem] * 2 + [vmem] * 8,
        out_specs=(vmem,) * 5,
        scratch_shapes=[state] * 6
        + [
            pltpu.VMEM((tok, width), F32),
            pltpu.VMEM((tok, width), F32),
            pltpu.VMEM((tok, width), F32),
            pltpu.VMEM((nb, tok, LANES), BF16),
            pltpu.VMEM((tok, width), BF16),
            pltpu.VMEM((6, tok, LANES), F32),
            pltpu.VMEM((4, tok, tok), F32),
            pltpu.VMEM((7, tok, LANES), F32),
            pltpu.VMEM((nb, 8, LANES), F32),
            pltpu.VMEM((nb, 8, LANES), F32),
            pltpu.VMEM((nb, 8, LANES), F32),
            pltpu.VMEM((LANES, tok), BF16),
            pltpu.VMEM((LANES, tok), BF16),
            pltpu.VMEM((7, 8, LANES), F32),
            pltpu.VMEM((zr, rows, LANES), F32),
            pltpu.VMEM((xr, rows, LANES), F32),
            pltpu.VMEM((dpn, rows, LANES), F32),
        ]
        + [dma((nb * SPLIT,))] * 4
        + [dma((4,)), dma((4,)), dma((zr,)), dma((zr,)), dma((xr,)), dma((xr,)), dma((dpn,)), dma((dpn,))],
        compiler_params=pltpu.CompilerParams(
            collective_id=0, has_side_effects=True, vmem_limit_bytes=52 * 1024 * 1024
        ),
        name="mixer",
    )(
        log_rates, skips, inputs[0], gates[0], targets[0], keys_b[0], reads_c[0],
        step_codes, seg_starts, gains.reshape(1, width),
    )
    tail = red[nb:]
    heads = lambda base: tail[:, base : base + nb // 4].reshape(8, nb // 8, 2).transpose(1, 0, 2).reshape(2 * nb)
    return (
        jnp.sum(tail[:, 127]), gx[None], gz[None], gb[None], gc[None],
        heads(0), heads(64), red[:nb].reshape(width),
    )


def solution(mesh):
    wide, line = P("dp", "seq", None), P("dp", "seq")
    return jax.shard_map(
        functools.partial(shards, mesh),
        mesh=mesh,
        in_specs=(wide, wide, wide, wide, line, line, wide, P(), P(), P()),
        out_specs=(P(), wide, wide, wide, wide, P(), P(), P()),
        check_vma=False,
    )
```

```python
import functools

import jax
import jax.numpy as jnp
from jax import lax
from jax.experimental import pallas as pl
from jax.experimental.pallas import tpu as pltpu
from jax.sharding import PartitionSpec as P

F32, BF16 = jnp.float32, jnp.bfloat16
LANES = 128
Z_RING = 8
SPLIT = 4
LAG = (20, 8)


def red8(v):
    return v.reshape(v.shape[0] // 8, 8, LANES).sum(axis=0)


def mm(a, b):
    return lax.dot_general(a, b, (((1,), (0,)), ((), ())), preferred_element_type=F32)


def mm_nt(a, b):
    return lax.dot_general(a, b, (((1,), (1,)), ((), ())), preferred_element_type=F32)


def mm_tn(a, b):
    return lax.dot_general(a, b, (((0,), (0,)), ((), ())), preferred_element_type=F32)


def kernel(
    xr, zr, dpn, nb, rows_total,
    lr, sk, x_in, z_in, tg_in, bk, ck, codes, segs, gains,
    gx, gz, gb, gc, red, red_rates,
    x, z, tg,
    s_st, p_st, k_st, d_st, r_st, q_st,
    mix, ebuf, dxa, inter, ub,
    cols, tab, acc, ga, sa, ra, bt, ct, meta,
    wide_bufs, rate_bufs,
    f_recv, f_carry, b_recv, b_carry, sends, msems, local,
    wide_sems, rate_sems,
):
    tok = x.shape[0]
    width = nb * LANES
    me, dpi = lax.axis_index("seq"), lax.axis_index("dp")
    zi, xi = lax.rem(me, zr), lax.div(me, zr)
    z_at = lambda k: {"seq": xi * zr + lax.rem(zi + k, zr)}
    x_at = lambda k: {"seq": lax.rem(xi + k, xr) * zr + zi}
    d_at = lambda k: {"dp": lax.rem(dpi + k, dpn)}

    barrier = pltpu.get_barrier_semaphore()
    peers = [z_at(k) for k in range(1, zr)] + [x_at(k) for k in range(1, xr)] + [d_at(k) for k in range(1, dpn)]
    for peer in peers:
        pl.semaphore_signal(barrier, inc=1, device_id=peer, device_id_type=pl.DeviceIdType.MESH)

    loads = [pltpu.make_async_copy(src, dst, local.at[i]) for i, (src, dst) in enumerate(((x_in, x), (z_in, z), (tg_in, tg)))]
    for load in loads:
        load.start()

    t_i = lax.broadcasted_iota(jnp.int32, (tok, tok), 0)
    s_i = lax.broadcasted_iota(jnp.int32, (tok, tok), 1)
    diag, upto = t_i == s_i, s_i <= t_i

    def forms(row):
        wide = jnp.broadcast_to(row, (tok, tok))
        own = jnp.sum(jnp.where(diag, wide, 0.0), axis=1, keepdims=True)
        col = jnp.sum(jnp.where(upto, wide, 0.0), axis=1, keepdims=True)
        across = jnp.sum(jnp.where(t_i <= s_i, jnp.broadcast_to(own, (tok, tok)), 0.0), axis=0, keepdims=True)
        return own, col, across, jnp.sum(row, axis=1, keepdims=True)

    code_row = codes[...].astype(F32)
    code_own, cum_col, cum_row, cum_end = forms(code_row)
    _, seg_col, seg_row, seg_end = forms(segs[...].astype(F32))
    visible = upto & (seg_col == seg_row)
    c_mat, b_mat = ck[...], bk[...]
    dt_row = code_row * (1.0 / 64.0)
    gap = jnp.where(visible, (cum_col - cum_row) * (1.0 / 64.0), 0.0)
    dt_vis = jnp.where(visible, jnp.broadcast_to(dt_row, (tok, tok)), 0.0)
    cb_dt = mm_nt(c_mat, b_mat) * dt_vis
    tab[0], tab[1], tab[2], tab[3] = gap, cb_dt, cb_dt * gap, dt_vis
    shape = (tok, LANES)
    cols[0] = jnp.broadcast_to(cum_col * (1.0 / 64.0), shape)
    cols[1] = jnp.broadcast_to((cum_end - cum_col) * (1.0 / 64.0), shape)
    cols[2] = jnp.broadcast_to(jnp.where(seg_col == seg_end, code_own * (1.0 / 64.0), 0.0), shape)
    cols[3] = jnp.broadcast_to((seg_col == 0.0).astype(F32), shape)
    bt[...], ct[...] = b_mat.astype(F32).T.astype(BF16), c_mat.astype(F32).T.astype(BF16)
    end_dt = jnp.broadcast_to(cum_end * (1.0 / 64.0), (1, LANES))
    broken = jnp.broadcast_to((seg_end > 0.0).astype(F32), (1, LANES))
    meta[6] = jnp.where(
        lax.broadcasted_iota(jnp.int32, (8, LANES), 0) == 0, end_dt,
        jnp.where(lax.broadcasted_iota(jnp.int32, (8, LANES), 0) == 1, broken, 0.0),
    )
    acc[...] = jnp.zeros_like(acc)

    low = lax.broadcasted_iota(jnp.int32, (1, LANES), 1) < LANES // 2

    def rates(b):
        a0 = jnp.exp(jnp.full((1, LANES), lr[2 * b], F32))
        a1 = jnp.exp(jnp.full((1, LANES), lr[2 * b + 1], F32))
        return a0, a1, jnp.where(low, a0, a1)

    def skip_row(b):
        return jnp.where(low, jnp.full((1, LANES), sk[2 * b], F32), jnp.full((1, LANES), sk[2 * b + 1], F32))

    def decay_of(m, a):
        return jnp.where(m[1:2] > 0.0, 0.0, jnp.exp(-a * m[0:1]))

    def lanes(b):
        return pl.ds(pl.multiple_of(b * LANES, LANES), LANES)

    def pair(b):
        xb = x[:, lanes(b)]
        zero = jnp.zeros_like(xb)
        return jnp.concatenate([jnp.where(low, xb, zero), jnp.where(low, zero, xb)], axis=0)

    part = tok // SPLIT

    class Pass:
        def __init__(self, pos, row, up, down, across, out, recv, carry, recv_sem, carry_sem, sem0):
            self.pos, self.row, self.up, self.down, self.across = pos, row, up, down, across
            self.out, self.recv, self.carry = out, recv, carry
            self.recv_sem, self.carry_sem, self.sem0 = recv_sem, carry_sem, sem0
            self.lag = jnp.where(row == 0, 0, lax.div((2 * (zr - 1) + row - 2 * pos) * LAG[0], LAG[1]))

        def copy(self, src, dst, b, q, send, recv, to):
            cut = (b, pl.ds(q * part, part))
            return pltpu.make_async_remote_copy(
                src_ref=src.at[cut], dst_ref=dst.at[cut], send_sem=sends.at[self.sem0 + send],
                recv_sem=recv.at[b * SPLIT + q], device_id=to, device_id_type=pl.DeviceIdType.MESH,
            )

        def head(self):
            m = self.sem0
            move = pltpu.make_async_remote_copy(
                src_ref=meta.at[m + 1], dst_ref=meta.at[m], send_sem=msems.at[m], recv_sem=msems.at[m + 1],
                device_id=self.up, device_id_type=pl.DeviceIdType.MESH,
            )

            @pl.when(self.pos == 0)
            def _():
                meta[m] = jnp.zeros((8, LANES), F32)

            @pl.when(self.pos > 0)
            def _():
                move.wait_recv()

            meta[m + 1] = meta[m] + meta[6]

            @pl.when(self.pos < zr - 1)
            def _():
                move.start()

            return move

        def scan(self, b):
            _, _, a = rates(b)
            g = decay_of(meta[6], a)
            for q in range(SPLIT):
                cut = (b, pl.ds(q * part, part))
                move = self.copy(self.out, self.recv, b, q, 0, self.recv_sem, self.up)

                @pl.when(self.pos > 0)
                def _():
                    move.wait_recv()
                    self.out[cut] = self.out[cut] + g * self.recv[cut]

                @pl.when(self.pos == 0)
                def _():
                    self.recv[cut] = jnp.zeros((part, LANES), F32)

                @pl.when(self.pos < zr - 1)
                def _():
                    move.start()

        def take(self, b):
            _, _, a = rates(b)
            for q in range(SPLIT):
                cut = (b, pl.ds(q * part, part))
                onward = self.copy(self.carry, self.carry, b, q, 1, self.carry_sem, self.down)

                @pl.when(self.row > 0)
                def _():
                    onward.wait_recv()

                    @pl.when(self.pos > 0)
                    def _():
                        onward.start()

                @pl.when((self.pos == zr - 1) & (self.row < xr - 1))
                def _():
                    @pl.when(self.row > 0)
                    def _():
                        self.out[cut] = self.out[cut] + decay_of(meta[self.sem0 + 1], a) * self.carry[cut]

                    self.copy(self.out, self.carry, b, q, 0, self.carry_sem, self.across).start()

                @pl.when(self.row > 0)
                def _():
                    self.recv[cut] = self.recv[cut] + decay_of(meta[self.sem0], a) * self.carry[cut]

        def finish(self, move):
            @pl.when(self.pos < zr - 1)
            def _():
                move.wait_send()

            whole = lambda src, send, recv: pltpu.make_async_remote_copy(
                src_ref=src, dst_ref=src, send_sem=sends.at[self.sem0 + send], recv_sem=recv.at[0],
                device_id=self.up, device_id_type=pl.DeviceIdType.MESH,
            )

            @pl.when((self.pos < zr - 1) | (self.row < xr - 1))
            def _():
                whole(self.out, 0, self.recv_sem).wait_send()

            @pl.when((self.row > 0) & (self.pos > 0))
            def _():
                whole(self.carry, 1, self.carry_sem).wait_send()

        def run(self, make, beside, then, made=None):
            def step(i, carry):
                @pl.when(i < nb)
                def _():
                    make(i)
                    self.scan(i)
                    beside(i)

                if made is not None:
                    @pl.when(i == nb - 1)
                    def _():
                        made()

                @pl.when(i >= self.lag)
                def _():
                    self.take(i - self.lag)
                    then(i - self.lag)

                return carry

            lax.fori_loop(0, nb + self.lag, step, 0)

    fwd = Pass(zi, xi, z_at(1), z_at(zr - 1), x_at(1), s_st, p_st, k_st, f_recv, f_carry, 0)
    bwd = Pass(zr - 1 - zi, xr - 1 - xi, z_at(zr - 1), z_at(1), x_at(xr - 1), d_st, r_st, q_st, b_recv, b_carry, 2)

    def block_state(b):
        _, _, a = rates(b)
        u = (x[:, lanes(b)].astype(F32) * (jnp.exp(-a * cols[1]) * cols[2])).astype(BF16)
        ub[:, lanes(b)] = u
        s_st[b] = mm(bt[...], u)

    def scores_of(b):
        a0, a1, _ = rates(b)
        gap, cbd = tab[0], tab[1]
        e0, e1 = jnp.exp(-a0 * gap), jnp.exp(-a1 * gap)
        both = jnp.concatenate([(cbd * e0).astype(BF16), (cbd * e1).astype(BF16)], axis=1)
        return e0, e1, both

    def inside(b):
        _, _, both = scores_of(b)
        mix[:, lanes(b)] = mm(both, pair(b)) + skip_row(b) * x[:, lanes(b)].astype(F32)

    def mixture(b):
        _, _, a = rates(b)
        at = lanes(b)
        state = p_st[b].astype(BF16)
        inter[b] = state
        e = mm(c_mat_ref[...], state)
        ebuf[:, at] = e
        m = mix[:, at] + jnp.exp(-a * cols[0]) * cols[3] * e
        mix[:, at] = m
        zf = z[:, at].astype(F32)
        gated = m * (zf / (1.0 + jnp.exp(-zf)))
        gg = gated * gains[:, at]
        acc[0] += gated * gated
        acc[1] += gg * gg
        acc[2] += gg * tg[:, at].astype(F32)

    c_mat_ref, b_mat_ref = ck, bk

    for load in loads:
        load.wait()
    pl.semaphore_wait(barrier, len(peers))
    first = fwd.head()
    fwd.run(block_state, inside, mixture)

    squares = jnp.sum(acc[0], axis=1, keepdims=True)
    r_col = lax.rsqrt(squares * (1.0 / width) + 1e-5)
    coef = r_col * r_col * r_col * (1.0 / width) * (
        r_col * jnp.sum(acc[1], axis=1, keepdims=True) - jnp.sum(acc[2], axis=1, keepdims=True)
    )
    cols[4] = jnp.broadcast_to(r_col, shape)
    cols[5] = jnp.broadcast_to(coef, shape)

    def direct(b):
        _, _, a = rates(b)
        at = lanes(b)
        m, xf, zf, gain, r = mix[:, at], x[:, at].astype(F32), z[:, at].astype(F32), gains[:, at], cols[4]
        sig = 1.0 / (1.0 + jnp.exp(-zf))
        sg = zf * sig
        gated = m * sg
        unit = gated * r
        miss = unit * gain - tg[:, at].astype(F32)
        dgated = r * (miss * gain) - gated * cols[5]
        dmix = dgated * sg
        de = jnp.exp(-a * cols[0]) * cols[3] * dmix
        deb = de.astype(BF16)
        d_st[b] = mm(ct[...], deb)
        mix[:, at] = dmix
        gz[:, at] = (dgated * m * (sig * (1.0 + zf * (1.0 - sig)))).astype(BF16)
        acc[3, 0:8] += red8(miss * miss)
        ga[b] = red8(miss * unit)
        sa[b] = red8(dmix * xf)
        ra[b] = red8(cols[0] * de * ebuf[:, at])
        acc[4] += mm_nt(deb, inter[b])

    def inside_back(b):
        at = lanes(b)
        e0, e1, both = scores_of(b)
        dmix = mix[:, at]
        dmb = dmix.astype(BF16)
        ds = mm_nt(dmb, pair(b))
        d0, d1 = ds[:, :tok] * e0, ds[:, tok:] * e1
        acc[5] += d0 + d1
        v0, v1 = red8(d0 * tab[2]), red8(d1 * tab[2])
        ra[b] += jnp.where(low, v0 + pltpu.roll(v0, LANES // 2, 1), v1 + pltpu.roll(v1, LANES // 2, 1))
        back = mm_tn(both, dmb)
        dxa[:, at] = jnp.where(low, back[:tok], back[tok:]) + skip_row(b) * dmix

    def state_back(b):
        _, _, a = rates(b)
        at = lanes(b)
        by = r_st[b]
        byb = by.astype(BF16)
        duw = mm(b_mat_ref[...], byb) * (jnp.exp(-a * cols[1]) * cols[2])
        gx[:, at] = (dxa[:, at] + duw).astype(BF16)
        own = meta[6]
        ra[b] += red8(cols[1] * duw * x[:, at].astype(F32)) + red8(by * p_st[b]) * (own[0:1] * decay_of(own, a))
        acc[6] += mm_nt(ub[:, at], byb)

    lane8 = lax.broadcasted_iota(jnp.int32, (8, LANES), 1)
    row8 = lax.broadcasted_iota(jnp.int32, (8, LANES), 0)

    def by_head(rows):
        h0 = jnp.sum(jnp.where(low, rows, 0.0), axis=1, keepdims=True)
        h1 = jnp.sum(jnp.where(low, 0.0, rows), axis=1, keepdims=True)
        tile = jnp.zeros((8, LANES), F32)
        for g in range(nb // 8):
            cut, lane = slice(8 * g, 8 * g + 8), 16 * g + 2 * row8
            tile += jnp.where(lane8 == lane, h0[cut], 0.0) + jnp.where(lane8 == lane + 1, h1[cut], 0.0)
        return tile

    class Stage:
        def __init__(self, buf, sems, axis):
            self.buf, self.ss, self.rs = buf, sems[0], sems[1]
            self.mine, self.n, self.at = ((zi, zr, z_at), (xi, xr, x_at), (dpi, dpn, d_at))[axis]

        def hop(self, k, slot):
            return pltpu.make_async_remote_copy(
                src_ref=self.buf.at[slot], dst_ref=self.buf.at[slot], send_sem=self.ss.at[k], recv_sem=self.rs.at[k],
                device_id=self.at(k), device_id_type=pl.DeviceIdType.MESH,
            )

        def start(self, total):
            self.buf[self.mine] = total
            for k in range(1, self.n):
                self.hop(k, self.mine).start()

        def result(self):
            for k in range(1, self.n):
                self.hop(k, lax.rem(self.mine + self.n - k, self.n)).wait_recv()
            total = self.buf[0]
            for k in range(1, self.n):
                total = total + self.buf[k]
            return total

        def close(self):
            for k in range(1, self.n):
                self.hop(k, self.mine).wait_send()

    w_stage = [Stage(wide_bufs[i], wide_sems[i], i) for i in range(3)]
    r_stage = [Stage(rate_bufs[i], rate_sems[i], i) for i in range(3)]

    def early_sums():
        lost = 0.5 * jnp.sum(acc[3, 0:8], axis=1, keepdims=True)
        tile = by_head(sa[...].sum(axis=1)) + jnp.where(lane8 == LANES - 1, lost, 0.0)
        w_stage[0].start(jnp.concatenate([ga[...].sum(axis=1), tile], axis=0))

    second = bwd.head()
    bwd.run(direct, inside_back, state_back, early_sums)

    a_rows = jnp.concatenate([rates(b)[2] for b in range(nb)], axis=0)
    r_stage[0].start(by_head(ra[...].sum(axis=1) * -a_rows))
    w_stage[1].start(w_stage[0].result())
    dcb = (acc[5] * tab[3]).astype(BF16)
    gc[...] = (acc[4] + mm(dcb, bk[...])).astype(BF16)
    gb[...] = (acc[6] + mm_tn(dcb, ck[...])).astype(BF16)
    r_stage[1].start(r_stage[0].result())
    w_stage[2].start(w_stage[1].result())
    r_stage[2].start(r_stage[1].result())
    red[...] = w_stage[2].result() * (1.0 / rows_total)
    fwd.finish(first)
    bwd.finish(second)
    for stage in w_stage + r_stage[:2]:
        stage.close()
    red_rates[...] = r_stage[2].result() * (1.0 / rows_total)
    r_stage[2].close()


def hand_over(nb, gx, gz, gb, gc, red, red_rates, gx_out, gz_out, gb_out, gc_out, loss, rate, skip, gain, sems):
    moves = [pltpu.make_async_copy(a, b, sems.at[i]) for i, (a, b) in enumerate(((gx, gx_out), (gz, gz_out)))]
    for move in moves:
        move.start()
    gb_out[...] = gb[...]
    gc_out[...] = gc[...]
    for b in range(nb):
        gain[:, b * LANES : (b + 1) * LANES] = red[b : b + 1, :]
    tail = jnp.sum(red[nb:, :], axis=0, keepdims=True)
    loss[...] = tail[:, LANES - 1 :]
    skip[...] = tail[:, : 2 * nb]
    rate[...] = jnp.sum(red_rates[...], axis=0, keepdims=True)[:, : 2 * nb]
    for move in moves:
        move.wait()


def shards(mesh, inputs, gates, keys_b, reads_c, step_codes, seg_starts, targets, log_rates, skips, gains):
    tok, width = inputs.shape[1:]
    nb = width // LANES
    seq, dpn = mesh.shape["seq"], mesh.shape["dp"]
    zr = min(Z_RING, seq)
    xr = seq // zr
    vmem, smem = pl.BlockSpec(memory_space=pltpu.VMEM), pl.BlockSpec(memory_space=pltpu.SMEM)
    hbm = pl.BlockSpec(memory_space=pltpu.HBM)
    rows = nb + 8
    state = pltpu.VMEM((nb, tok, LANES), F32)
    dma = pltpu.SemaphoreType.DMA
    counts = (zr, xr, dpn)
    of = jax.ShapeDtypeStruct
    wide, small = of((tok, width), BF16), of(keys_b.shape[1:], BF16)
    flat, half = pltpu.VMEM((tok, width), F32), pltpu.VMEM((tok, width), BF16)
    results = pl.pallas_call(
        functools.partial(kernel, xr, zr, dpn, nb, float(tok * seq * dpn)),
        out_shape=(wide, wide, small, small, of((rows, LANES), F32), of((8, LANES), F32)),
        in_specs=[smem] * 2 + [hbm] * 3 + [vmem] * 5,
        out_specs=(vmem,) * 6,
        scratch_shapes=[half] * 3
        + [state] * 6
        + [
            flat,
            flat,
            flat,
            pltpu.VMEM((nb, tok, LANES), BF16),
            half,
            pltpu.VMEM((6, tok, LANES), F32),
            pltpu.VMEM((4, tok, tok), F32),
            pltpu.VMEM((7, tok, LANES), F32),
            pltpu.VMEM((nb, 8, LANES), F32),
            pltpu.VMEM((nb, 8, LANES), F32),
            pltpu.VMEM((nb, 8, LANES), F32),
            pltpu.VMEM((LANES, tok), BF16),
            pltpu.VMEM((LANES, tok), BF16),
            pltpu.VMEM((7, 8, LANES), F32),
            [pltpu.VMEM((n, rows, LANES), F32) for n in counts],
            [pltpu.VMEM((n, 8, LANES), F32) for n in counts],
        ]
        + [dma((nb * SPLIT,))] * 4
        + [dma((4,)), dma((4,)), dma((3,))]
        + [[[dma((n,)), dma((n,))] for n in counts] for _ in range(2)],
        compiler_params=pltpu.CompilerParams(
            collective_id=0, has_side_effects=True, vmem_limit_bytes=56 * 1024 * 1024
        ),
        name="mixer",
    )(
        log_rates, skips, inputs[0], gates[0], targets[0], keys_b[0], reads_c[0],
        step_codes, seg_starts, gains.reshape(1, width),
    )
    line = of((1, 2 * nb), F32)
    gx, gz, gb, gc, loss, rate, skip, gain = pl.pallas_call(
        functools.partial(hand_over, nb),
        out_shape=(wide, wide, small, small, of((1, 1), F32), line, line, of((1, width), F32)),
        in_specs=[vmem] * 6,
        out_specs=(hbm,) * 2 + (vmem,) * 6,
        scratch_shapes=[dma((2,))],
        name="hand_over",
    )(*results)
    return (
        loss[0, 0], gx[None], gz[None], gb[None], gc[None], rate[0], skip[0], gain[0],
    )


def solution(mesh):
    wide, line = P("dp", "seq", None), P("dp", "seq")
    return jax.shard_map(
        functools.partial(shards, mesh),
        mesh=mesh,
        in_specs=(wide, wide, wide, wide, line, line, wide, P(), P(), P()),
        out_specs=(P(), wide, wide, wide, wide, P(), P(), P()),
        check_vma=False,
    )
```

```python
import functools

import jax
import jax.numpy as jnp
from jax import lax
from jax.experimental import pallas as pl
from jax.experimental.pallas import tpu as pltpu
from jax.sharding import PartitionSpec as P

F32, BF16 = jnp.float32, jnp.bfloat16
LANES = 128
Z_RING = 8
SPLIT = 2
HOP = (21, 8)


def red8(v):
    return v.reshape(v.shape[0] // 8, 8, LANES).sum(axis=0)


def mm(a, b):
    return lax.dot_general(a, b, (((1,), (0,)), ((), ())), preferred_element_type=F32)


def mm_nt(a, b):
    return lax.dot_general(a, b, (((1,), (1,)), ((), ())), preferred_element_type=F32)


def mm_tn(a, b):
    return lax.dot_general(a, b, (((0,), (0,)), ((), ())), preferred_element_type=F32)


def kernel(
    xr, zr, dpn, nb, rows_total,
    lr, sk, x_in, z_in, tg_in, bk, ck, codes, segs, gains,
    gx, gz, gb, gc, red, red_rates,
    x, z, tg,
    f_out, p_st, f_carry, f_part, b_out, r_st, b_carry, b_part,
    mix, ebuf, dxa, inter, ub,
    cols, tab, acc, ga, sa, ra, bt, ct, meta, row_meta,
    wide_bufs, rate_bufs,
    recv_sems, sends, local,
    wide_sems, rate_sems, meta_sems,
):
    tok = x.shape[0]
    width = nb * LANES
    me, dpi = lax.axis_index("seq"), lax.axis_index("dp")
    zi, xi = lax.rem(me, zr), lax.div(me, zr)
    z_at = lambda k: {"seq": xi * zr + lax.rem(zi + k, zr)}
    x_at = lambda k: {"seq": lax.rem(xi + k, xr) * zr + zi}
    d_at = lambda k: {"dp": lax.rem(dpi + k, dpn)}

    barrier = pltpu.get_barrier_semaphore()
    peers = [z_at(k) for k in range(1, zr)] + [x_at(k) for k in range(1, xr)] + [d_at(k) for k in range(1, dpn)]
    for peer in peers:
        pl.semaphore_signal(barrier, inc=1, device_id=peer, device_id_type=pl.DeviceIdType.MESH)

    loads = [pltpu.make_async_copy(src, dst, local.at[i]) for i, (src, dst) in enumerate(((x_in, x), (z_in, z), (tg_in, tg)))]
    for load in loads:
        load.start()

    t_i = lax.broadcasted_iota(jnp.int32, (tok, tok), 0)
    s_i = lax.broadcasted_iota(jnp.int32, (tok, tok), 1)
    diag, upto = t_i == s_i, s_i <= t_i

    def forms(row):
        wide = jnp.broadcast_to(row, (tok, tok))
        own = jnp.sum(jnp.where(diag, wide, 0.0), axis=1, keepdims=True)
        col = jnp.sum(jnp.where(upto, wide, 0.0), axis=1, keepdims=True)
        across = jnp.sum(jnp.where(t_i <= s_i, jnp.broadcast_to(own, (tok, tok)), 0.0), axis=0, keepdims=True)
        return own, col, across, jnp.sum(row, axis=1, keepdims=True)

    code_row = codes[...].astype(F32)
    code_own, cum_col, cum_row, cum_end = forms(code_row)
    _, seg_col, seg_row, seg_end = forms(segs[...].astype(F32))
    visible = upto & (seg_col == seg_row)
    c_mat, b_mat = ck[...], bk[...]
    dt_row = code_row * (1.0 / 64.0)
    gap = jnp.where(visible, (cum_col - cum_row) * (1.0 / 64.0), 0.0)
    dt_vis = jnp.where(visible, jnp.broadcast_to(dt_row, (tok, tok)), 0.0)
    cb_dt = mm_nt(c_mat, b_mat) * dt_vis
    tab[0], tab[1], tab[2], tab[3] = gap, cb_dt, cb_dt * gap, dt_vis
    shape = (tok, LANES)
    cols[0] = jnp.broadcast_to(cum_col * (1.0 / 64.0), shape)
    cols[1] = jnp.broadcast_to((cum_end - cum_col) * (1.0 / 64.0), shape)
    cols[2] = jnp.broadcast_to(jnp.where(seg_col == seg_end, code_own * (1.0 / 64.0), 0.0), shape)
    cols[3] = jnp.broadcast_to((seg_col == 0.0).astype(F32), shape)
    bt[...], ct[...] = b_mat.astype(F32).T.astype(BF16), c_mat.astype(F32).T.astype(BF16)
    end_dt = jnp.broadcast_to(cum_end * (1.0 / 64.0), (1, LANES))
    broken = jnp.broadcast_to((seg_end > 0.0).astype(F32), (1, LANES))
    meta[10] = jnp.where(
        lax.broadcasted_iota(jnp.int32, (8, LANES), 0) == 0, end_dt,
        jnp.where(lax.broadcasted_iota(jnp.int32, (8, LANES), 0) == 1, broken, 0.0),
    )
    acc[...] = jnp.zeros_like(acc)

    low = lax.broadcasted_iota(jnp.int32, (1, LANES), 1) < LANES // 2

    def rates(b):
        a0 = jnp.exp(jnp.full((1, LANES), lr[2 * b], F32))
        a1 = jnp.exp(jnp.full((1, LANES), lr[2 * b + 1], F32))
        return a0, a1, jnp.where(low, a0, a1)

    def skip_row(b):
        return jnp.where(low, jnp.full((1, LANES), sk[2 * b], F32), jnp.full((1, LANES), sk[2 * b + 1], F32))

    def decay_of(m, a):
        return jnp.where(m[1:2] > 0.0, 0.0, jnp.exp(-a * m[0:1]))

    def lanes(b):
        return pl.ds(pl.multiple_of(b * LANES, LANES), LANES)

    def pair(b):
        xb = x[:, lanes(b)]
        zero = jnp.zeros_like(xb)
        return jnp.concatenate([jnp.where(low, xb, zero), jnp.where(low, zero, xb)], axis=0)

    part = tok // SPLIT

    class Stage:
        def __init__(self, buf, sems, axis):
            self.buf, self.ss, self.rs = buf, sems[0], sems[1]
            self.mine, self.n, self.at = ((zi, zr, z_at), (xi, xr, x_at), (dpi, dpn, d_at))[axis]

        def hop(self, k, slot):
            return pltpu.make_async_remote_copy(
                src_ref=self.buf.at[slot], dst_ref=self.buf.at[slot], send_sem=self.ss.at[k], recv_sem=self.rs.at[k],
                device_id=self.at(k), device_id_type=pl.DeviceIdType.MESH,
            )

        def start(self, total):
            self.buf[self.mine] = total
            for k in range(1, self.n):
                self.hop(k, self.mine).start()

        def result(self):
            for k in range(1, self.n):
                self.hop(k, lax.rem(self.mine + self.n - k, self.n)).wait_recv()
            total = self.buf[0]
            for k in range(1, self.n):
                total = total + self.buf[k]
            return total

        def close(self):
            for k in range(1, self.n):
                self.hop(k, self.mine).wait_send()

    half, mid = nb // 2, zr // 2
    ticks = lambda hops: lax.div(hops * HOP[0], HOP[1])

    class Pass:
        def __init__(self, backward, out, recv, carry, partial):
            self.p = zr - 1 - zi if backward else zi
            self.r = xr - 1 - xi if backward else xi
            self.up, self.down = (z_at(zr - 1), z_at(1)) if backward else (z_at(1), z_at(zr - 1))
            self.across = x_at(xr - 1) if backward else x_at(1)
            self.out, self.recv, self.carry, self.part = out, recv, carry, partial
            self.base, self.backward = 5 * backward, backward
            self.sems = recv_sems[3 * backward : 3 * backward + 3]
            p, r = self.p, self.r
            self.low, self.high = p < mid, p >= mid
            self.first = [
                ticks(jnp.where(p < mid, p, zr - 1 - p)),
                ticks(jnp.where(p < mid, mid - 1 - p, p - mid)),
            ]
            self.second = [
                ticks(jnp.where(p < mid, jnp.where(r > 0, zr + r - p, p), r + p)),
                ticks(jnp.where(p < mid, mid + r + p, mid + r + zr - p)),
            ]

        def place_meta(self):
            slots = range(zr)
            at = lambda slot: zr - 1 - slot if self.backward else slot
            same = lambda q: self.low if q < mid else self.high
            rules = (
                lambda q: same(q) & (q < self.p),
                lambda q: same(q) & (q > self.p),
                lambda q: q < mid,
                lambda q: q >= mid,
                lambda q: True,
            )
            for n, rule in enumerate(rules):
                total = jnp.zeros((8, LANES), F32)
                for slot in slots:
                    total = total + jnp.where(rule(at(slot)), 1.0, 0.0) * row_meta[slot]
                meta[self.base + n] = total

        def decay(self, n, b):
            return decay_of(meta[self.base + n], rates(b)[2])

        def own(self, b):
            return decay_of(meta[10], rates(b)[2])

        def copy(self, src, dst, b, q, send, kind, to):
            cut = (b, pl.ds(q * part, part))
            return pltpu.make_async_remote_copy(
                src_ref=src.at[cut], dst_ref=dst.at[cut], send_sem=sends.at[send],
                recv_sem=self.sems[kind].at[b * SPLIT + q], device_id=to, device_id_type=pl.DeviceIdType.MESH,
            )

        def moves(self, s, b, q):
            sem = 6 * self.backward + 3 * s
            out, recv, carry, partial = self.out, self.recv, self.carry, self.part
            wait_recv = lambda: self.copy(recv, recv, b, q, sem, 0, self.up).wait_recv()
            wait_carry = lambda: self.copy(carry, carry, b, q, sem, 1, self.up).wait_recv()
            wait_part = lambda: self.copy(partial, partial, b, q, sem, 2, self.up).wait_recv()
            send_up = lambda: self.copy(out, recv, b, q, sem, 0, self.up).start()
            carry_down = lambda: self.copy(carry, carry, b, q, sem + 1, 1, self.down).start()
            part_down = lambda: self.copy(partial, partial, b, q, sem + 2, 2, self.down).start()
            return wait_recv, wait_carry, wait_part, send_up, carry_down, part_down

        def middle_first(self, b):
            p, r = self.p, self.r
            g, above = self.own(b), self.decay(1, b)
            for q in range(SPLIT):
                cut = (b, pl.ds(q * part, part))
                wait_recv, _, wait_part, send_up, _, part_down = self.moves(0, b, q)

                @pl.when(p < mid)
                def _():
                    @pl.when(p > 0)
                    def _():
                        wait_recv()
                        self.out[cut] = self.out[cut] + g * self.recv[cut]

                    @pl.when(p == 0)
                    def _():
                        self.recv[cut] = jnp.zeros((part, LANES), F32)

                    send_up()

                @pl.when((p > mid) & (r < xr - 1))
                def _():
                    @pl.when(p < zr - 1)
                    def _():
                        wait_part()
                        self.part[cut] = self.part[cut] + above * self.out[cut]

                    @pl.when(p == zr - 1)
                    def _():
                        self.part[cut] = self.out[cut]

                    part_down()

        def ends_first(self, b):
            p, r = self.p, self.r
            g, above = self.own(b), self.decay(1, b)
            for q in range(SPLIT):
                cut = (b, pl.ds(q * part, part))
                wait_recv, _, wait_part, send_up, _, part_down = self.moves(1, b, q)
                to_end = lambda: self.copy(self.out, self.carry, b, q, 6 * self.backward + 3, 1, self.up).start()

                @pl.when(p < mid)
                def _():
                    @pl.when(p < mid - 1)
                    def _():
                        wait_part()
                        self.part[cut] = self.part[cut] + above * self.out[cut]

                    @pl.when(p == mid - 1)
                    def _():
                        self.part[cut] = self.out[cut]

                    @pl.when(p > 0)
                    def _():
                        part_down()

                @pl.when(p >= mid)
                def _():
                    @pl.when(p > mid)
                    def _():
                        wait_recv()
                        self.out[cut] = self.out[cut] + g * self.recv[cut]

                    @pl.when(p == mid)
                    def _():
                        self.recv[cut] = jnp.zeros((part, LANES), F32)

                    @pl.when(p < zr - 1)
                    def _():
                        send_up()

                    @pl.when((p == zr - 1) & (r < xr - 1))
                    def _():
                        to_end()

        def middle_second(self, b):
            p, r = self.p, self.r
            g = self.own(b)
            for q in range(SPLIT):
                cut = (b, pl.ds(q * part, part))
                wait_recv, wait_carry, wait_part, send_up, carry_down, _ = self.moves(0, b, q)
                onward = lambda: self.copy(self.part, self.carry, b, q, 6 * self.backward + 2, 1, self.across).start()

                @pl.when((p <= mid) & (r > 0))
                def _():
                    wait_carry()

                    @pl.when(p > 0)
                    def _():
                        carry_down()

                @pl.when((p < mid) & (r > 0))
                def _():
                    self.recv[cut] = self.recv[cut] + self.decay(0, b) * self.carry[cut]

                @pl.when(p >= mid)
                def _():
                    wait_recv()

                @pl.when(p == mid)
                def _():
                    @pl.when(r < xr - 1)
                    def _():
                        wait_part()
                        own = self.part[cut] + self.decay(1, b) * self.out[cut] + self.decay(3, b) * self.recv[cut]

                        @pl.when(r > 0)
                        def _():
                            self.part[cut] = own + self.decay(4, b) * self.carry[cut]

                        @pl.when(r == 0)
                        def _():
                            self.part[cut] = own

                        onward()

                    @pl.when(r > 0)
                    def _():
                        self.recv[cut] = self.recv[cut] + self.decay(2, b) * self.carry[cut]

                @pl.when((p >= mid) & (p < zr - 1))
                def _():
                    self.out[cut] = self.out[cut] + g * self.recv[cut]
                    send_up()

        def ends_second(self, b):
            p, r = self.p, self.r
            g = self.own(b)
            for q in range(SPLIT):
                cut = (b, pl.ds(q * part, part))
                wait_recv, wait_carry, _, send_up, carry_down, _ = self.moves(1, b, q)
                onward = lambda: self.copy(self.carry, self.recv, b, q, 6 * self.backward + 4, 0, self.across).start()
                to_end = lambda: self.copy(self.part, self.carry, b, q, 6 * self.backward + 5, 1, self.down).start()

                @pl.when((p < mid) & ((p > 0) | (r > 0)))
                def _():
                    wait_recv()

                @pl.when((p == 0) & (r == 0))
                def _():
                    self.recv[cut] = jnp.zeros((part, LANES), F32)

                @pl.when((p == 0) & (r < xr - 1))
                def _():
                    wait_carry()
                    self.carry[cut] = self.carry[cut] + self.decay(3, b) * self.part[cut] + self.decay(4, b) * self.recv[cut]
                    onward()

                @pl.when(p < mid - 1)
                def _():
                    self.out[cut] = self.out[cut] + g * self.recv[cut]
                    send_up()

                @pl.when(p == 0)
                def _():
                    self.part[cut] = self.part[cut] + self.decay(2, b) * self.recv[cut]
                    to_end()

                @pl.when(p >= mid)
                def _():
                    wait_carry()

                    @pl.when(p > mid)
                    def _():
                        carry_down()

                    self.recv[cut] = self.recv[cut] + self.decay(0, b) * self.carry[cut]

        def finish(self):
            p, r = self.p, self.r
            sent = (
                (p < zr - 1),
                (p <= mid) & (p > 0) & (r > 0),
                (p >= mid) & (r < xr - 1),
                (p != mid - 1) & ((p < zr - 1) | (r < xr - 1)),
                ((p == 0) & (r < xr - 1)) | (p > mid),
                (p < mid),
            )
            for n, did in enumerate(sent):
                src = (self.out, self.carry, self.part)[n % 3].at[pl.ds(n // 3 * half, half)]
                move = pltpu.make_async_remote_copy(
                    src_ref=src, dst_ref=src, send_sem=sends.at[6 * self.backward + n], recv_sem=self.sems[0].at[0],
                    device_id=self.up, device_id_type=pl.DeviceIdType.MESH,
                )

                @pl.when(did)
                def _():
                    move.wait_send()

        def run(self, make, beside, then, events):
            def tick(i, _):
                def early(s, _):
                    c = i - jnp.where(s == 0, self.first[0], self.first[1])

                    @pl.when((c >= 0) & (c < half))
                    def _():
                        b = s * half + c
                        make(b)

                        @pl.when(s == 0)
                        def _():
                            self.middle_first(b)

                        @pl.when(s == 1)
                        def _():
                            self.ends_first(b)

                        beside(b)

                    return 0

                def late(s, _):
                    c = i - jnp.where(s == 0, self.second[0], self.second[1])

                    @pl.when((c >= 0) & (c < half))
                    def _():
                        b = s * half + c

                        @pl.when(s == 0)
                        def _():
                            self.middle_second(b)

                        @pl.when(s == 1)
                        def _():
                            self.ends_second(b)

                        then(b)

                    return 0

                lax.fori_loop(0, 2, early, 0)
                for when, event in events:
                    @pl.when(i == when)
                    def _():
                        event()

                lax.fori_loop(0, 2, late, 0)
                return 0

            lax.fori_loop(0, half + jnp.maximum(self.second[0], self.second[1]), tick, 0)

    fwd = Pass(False, f_out, p_st, f_carry, f_part)
    bwd = Pass(True, b_out, r_st, b_carry, b_part)
    meta_stage = Stage(row_meta, meta_sems, 0)

    def take_meta():
        meta_stage.result()
        fwd.place_meta()
        bwd.place_meta()

    def block_state(b):
        _, _, a = rates(b)
        u = (x[:, lanes(b)].astype(F32) * (jnp.exp(-a * cols[1]) * cols[2])).astype(BF16)
        ub[:, lanes(b)] = u
        f_out[b] = mm(bt[...], u)

    def scores_of(b):
        a0, a1, _ = rates(b)
        gap, cbd = tab[0], tab[1]
        e0, e1 = jnp.exp(-a0 * gap), jnp.exp(-a1 * gap)
        both = jnp.concatenate([(cbd * e0).astype(BF16), (cbd * e1).astype(BF16)], axis=1)
        return e0, e1, both

    def inside(b):
        _, _, both = scores_of(b)
        mix[:, lanes(b)] = mm(both, pair(b)) + skip_row(b) * x[:, lanes(b)].astype(F32)

    def mixture(b):
        _, _, a = rates(b)
        at = lanes(b)
        state = p_st[b].astype(BF16)
        inter[b] = state
        e = mm(c_mat_ref[...], state)
        ebuf[:, at] = e
        m = mix[:, at] + jnp.exp(-a * cols[0]) * cols[3] * e
        mix[:, at] = m
        zf = z[:, at].astype(F32)
        gated = m * (zf / (1.0 + jnp.exp(-zf)))
        gg = gated * gains[:, at]
        acc[0] += gated * gated
        acc[1] += gg * gg
        acc[2] += gg * tg[:, at].astype(F32)

    c_mat_ref, b_mat_ref = ck, bk

    for load in loads:
        load.wait()
    pl.semaphore_wait(barrier, len(peers))
    meta_stage.start(meta[10])
    fwd.run(block_state, inside, mixture, [(1, take_meta)])

    squares = jnp.sum(acc[0], axis=1, keepdims=True)
    r_col = lax.rsqrt(squares * (1.0 / width) + 1e-5)
    coef = r_col * r_col * r_col * (1.0 / width) * (
        r_col * jnp.sum(acc[1], axis=1, keepdims=True) - jnp.sum(acc[2], axis=1, keepdims=True)
    )
    cols[4] = jnp.broadcast_to(r_col, shape)
    cols[5] = jnp.broadcast_to(coef, shape)

    def direct(b):
        _, _, a = rates(b)
        at = lanes(b)
        m, xf, zf, gain, r = mix[:, at], x[:, at].astype(F32), z[:, at].astype(F32), gains[:, at], cols[4]
        sig = 1.0 / (1.0 + jnp.exp(-zf))
        sg = zf * sig
        gated = m * sg
        unit = gated * r
        miss = unit * gain - tg[:, at].astype(F32)
        dgated = r * (miss * gain) - gated * cols[5]
        dmix = dgated * sg
        de = jnp.exp(-a * cols[0]) * cols[3] * dmix
        deb = de.astype(BF16)
        b_out[b] = mm(ct[...], deb)
        mix[:, at] = dmix
        gz[:, at] = (dgated * m * (sig * (1.0 + zf * (1.0 - sig)))).astype(BF16)
        acc[3, 0:8] += red8(miss * miss)
        ga[b] = red8(miss * unit)
        sa[b] = red8(dmix * xf)
        ra[b] = red8(cols[0] * de * ebuf[:, at])
        acc[4] += mm_nt(deb, inter[b])

    def inside_back(b):
        at = lanes(b)
        e0, e1, both = scores_of(b)
        dmix = mix[:, at]
        dmb = dmix.astype(BF16)
        ds = mm_nt(dmb, pair(b))
        d0, d1 = ds[:, :tok] * e0, ds[:, tok:] * e1
        acc[5] += d0 + d1
        v0, v1 = red8(d0 * tab[2]), red8(d1 * tab[2])
        ra[b] += jnp.where(low, v0 + pltpu.roll(v0, LANES // 2, 1), v1 + pltpu.roll(v1, LANES // 2, 1))
        back = mm_tn(both, dmb)
        dxa[:, at] = jnp.where(low, back[:tok], back[tok:]) + skip_row(b) * dmix

    def state_back(b):
        _, _, a = rates(b)
        at = lanes(b)
        by = r_st[b]
        byb = by.astype(BF16)
        duw = mm(b_mat_ref[...], byb) * (jnp.exp(-a * cols[1]) * cols[2])
        gx[:, at] = (dxa[:, at] + duw).astype(BF16)
        own = meta[10]
        ra[b] += red8(cols[1] * duw * x[:, at].astype(F32)) + red8(by * p_st[b]) * (own[0:1] * decay_of(own, a))
        acc[6] += mm_nt(ub[:, at], byb)

    lane8 = lax.broadcasted_iota(jnp.int32, (8, LANES), 1)
    row8 = lax.broadcasted_iota(jnp.int32, (8, LANES), 0)

    def by_head(rows):
        h0 = jnp.sum(jnp.where(low, rows, 0.0), axis=1, keepdims=True)
        h1 = jnp.sum(jnp.where(low, 0.0, rows), axis=1, keepdims=True)
        tile = jnp.zeros((8, LANES), F32)
        for g in range(nb // 8):
            cut, lane = slice(8 * g, 8 * g + 8), 16 * g + 2 * row8
            tile += jnp.where(lane8 == lane, h0[cut], 0.0) + jnp.where(lane8 == lane + 1, h1[cut], 0.0)
        return tile

    w_stage = [Stage(wide_bufs[i], wide_sems[i], i) for i in range(3)]
    r_stage = [Stage(rate_bufs[i], rate_sems[i], i) for i in range(3)]

    def early_sums():
        lost = 0.5 * jnp.sum(acc[3, 0:8], axis=1, keepdims=True)
        tile = by_head(sa[...].sum(axis=1)) + jnp.where(lane8 == LANES - 1, lost, 0.0)
        w_stage[0].start(jnp.concatenate([ga[...].sum(axis=1), tile], axis=0))

    bwd.run(direct, inside_back, state_back, [(half - 1 + jnp.maximum(bwd.first[0], bwd.first[1]), early_sums)])

    a_rows = jnp.concatenate([rates(b)[2] for b in range(nb)], axis=0)
    r_stage[0].start(by_head(ra[...].sum(axis=1) * -a_rows))
    w_stage[1].start(w_stage[0].result())
    dcb = (acc[5] * tab[3]).astype(BF16)
    gc[...] = (acc[4] + mm(dcb, bk[...])).astype(BF16)
    gb[...] = (acc[6] + mm_tn(dcb, ck[...])).astype(BF16)
    r_stage[1].start(r_stage[0].result())
    w_stage[2].start(w_stage[1].result())
    r_stage[2].start(r_stage[1].result())
    red[...] = w_stage[2].result() * (1.0 / rows_total)
    fwd.finish()
    bwd.finish()
    meta_stage.close()
    for stage in w_stage + r_stage[:2]:
        stage.close()
    red_rates[...] = r_stage[2].result() * (1.0 / rows_total)
    r_stage[2].close()


def hand_over(nb, gx, gz, gb, gc, red, red_rates, gx_out, gz_out, gb_out, gc_out, loss, rate, skip, gain, sems):
    moves = [pltpu.make_async_copy(a, b, sems.at[i]) for i, (a, b) in enumerate(((gx, gx_out), (gz, gz_out)))]
    for move in moves:
        move.start()
    gb_out[...] = gb[...]
    gc_out[...] = gc[...]
    for b in range(nb):
        gain[:, b * LANES : (b + 1) * LANES] = red[b : b + 1, :]
    tail = jnp.sum(red[nb:, :], axis=0, keepdims=True)
    loss[...] = tail[:, LANES - 1 :]
    skip[...] = tail[:, : 2 * nb]
    rate[...] = jnp.sum(red_rates[...], axis=0, keepdims=True)[:, : 2 * nb]
    for move in moves:
        move.wait()


def shards(mesh, inputs, gates, keys_b, reads_c, step_codes, seg_starts, targets, log_rates, skips, gains):
    tok, width = inputs.shape[1:]
    nb = width // LANES
    seq, dpn = mesh.shape["seq"], mesh.shape["dp"]
    zr = min(Z_RING, seq)
    xr = seq // zr
    vmem, smem = pl.BlockSpec(memory_space=pltpu.VMEM), pl.BlockSpec(memory_space=pltpu.SMEM)
    hbm = pl.BlockSpec(memory_space=pltpu.HBM)
    rows = nb + 8
    state = pltpu.VMEM((nb, tok, LANES), F32)
    dma = pltpu.SemaphoreType.DMA
    counts = (zr, xr, dpn)
    of = jax.ShapeDtypeStruct
    wide, small = of((tok, width), BF16), of(keys_b.shape[1:], BF16)
    flat, half = pltpu.VMEM((tok, width), F32), pltpu.VMEM((tok, width), BF16)
    results = pl.pallas_call(
        functools.partial(kernel, xr, zr, dpn, nb, float(tok * seq * dpn)),
        out_shape=(wide, wide, small, small, of((rows, LANES), F32), of((8, LANES), F32)),
        in_specs=[smem] * 2 + [hbm] * 3 + [vmem] * 5,
        out_specs=(vmem,) * 6,
        scratch_shapes=[half] * 3
        + [state] * 8
        + [
            flat,
            flat,
            flat,
            pltpu.VMEM((nb, tok, LANES), BF16),
            half,
            pltpu.VMEM((6, tok, LANES), F32),
            pltpu.VMEM((4, tok, tok), F32),
            pltpu.VMEM((7, tok, LANES), F32),
            pltpu.VMEM((nb, 8, LANES), F32),
            pltpu.VMEM((nb, 8, LANES), F32),
            pltpu.VMEM((nb, 8, LANES), F32),
            pltpu.VMEM((LANES, tok), BF16),
            pltpu.VMEM((LANES, tok), BF16),
            pltpu.VMEM((11, 8, LANES), F32),
            pltpu.VMEM((zr, 8, LANES), F32),
            [pltpu.VMEM((n, rows, LANES), F32) for n in counts],
            [pltpu.VMEM((n, 8, LANES), F32) for n in counts],
        ]
        + [[dma((nb * SPLIT,))] * 6, dma((12,)), dma((3,))]
        + [[[dma((n,)), dma((n,))] for n in counts] for _ in range(2)]
        + [[dma((zr,)), dma((zr,))]],
        compiler_params=pltpu.CompilerParams(
            collective_id=0, has_side_effects=True, vmem_limit_bytes=56 * 1024 * 1024
        ),
        name="mixer",
    )(
        log_rates, skips, inputs[0], gates[0], targets[0], keys_b[0], reads_c[0],
        step_codes, seg_starts, gains.reshape(1, width),
    )
    line = of((1, 2 * nb), F32)
    gx, gz, gb, gc, loss, rate, skip, gain = pl.pallas_call(
        functools.partial(hand_over, nb),
        out_shape=(wide, wide, small, small, of((1, 1), F32), line, line, of((1, width), F32)),
        in_specs=[vmem] * 6,
        out_specs=(hbm,) * 2 + (vmem,) * 6,
        scratch_shapes=[dma((2,))],
        name="hand_over",
    )(*results)
    return (
        loss[0, 0], gx[None], gz[None], gb[None], gc[None], rate[0], skip[0], gain[0],
    )


def solution(mesh):
    wide, line = P("dp", "seq", None), P("dp", "seq")
    return jax.shard_map(
        functools.partial(shards, mesh),
        mesh=mesh,
        in_specs=(wide, wide, wide, wide, line, line, wide, P(), P(), P()),
        out_specs=(P(), wide, wide, wide, wide, P(), P(), P()),
        check_vma=False,
    )
```

```python
import functools

import jax
import jax.numpy as jnp
from jax import lax
from jax.experimental import pallas as pl
from jax.experimental.pallas import tpu as pltpu
from jax.sharding import PartitionSpec as P

F32, BF16 = jnp.float32, jnp.bfloat16
LANES = 128
Z_RING = 8
SPLIT = 2
HOP = (26, 8)
PIECES = 4


def red8(v):
    return v.reshape(v.shape[0] // 8, 8, LANES).sum(axis=0)


def mm(a, b):
    return lax.dot_general(a, b, (((1,), (0,)), ((), ())), preferred_element_type=F32)


def mm_nt(a, b):
    return lax.dot_general(a, b, (((1,), (1,)), ((), ())), preferred_element_type=F32)


def mm_tn(a, b):
    return lax.dot_general(a, b, (((0,), (0,)), ((), ())), preferred_element_type=F32)


def kernel(
    xr, zr, dpn, nb, rows_total,
    lr, sk, x_in, z_in, tg_in, bk, ck, codes, segs, gains,
    gx_out, gz_out, gb, gc, red, red_rates,
    x, z, tg, gx, gz,
    f_out, p_st, f_carry, f_part, b_out, r_st, b_carry, b_part,
    mix, ebuf, dxa, inter, ub,
    cols, tab, acc, ga, sa, ra, bt, ct, meta, row_meta,
    wide_bufs, rate_bufs,
    recv_sems, sends, local,
    wide_sems, rate_sems, meta_sems,
):
    tok = x.shape[0]
    width = nb * LANES
    me, dpi = lax.axis_index("seq"), lax.axis_index("dp")
    zi, xi = lax.rem(me, zr), lax.div(me, zr)
    z_at = lambda k: {"seq": xi * zr + lax.rem(zi + k, zr)}
    x_at = lambda k: {"seq": lax.rem(xi + k, xr) * zr + zi}
    d_at = lambda k: {"dp": lax.rem(dpi + k, dpn)}

    barrier = pltpu.get_barrier_semaphore()
    peers = [z_at(k) for k in range(1, zr)] + [x_at(k) for k in range(1, xr)] + [d_at(k) for k in range(1, dpn)]
    for peer in peers:
        pl.semaphore_signal(barrier, inc=1, device_id=peer, device_id_type=pl.DeviceIdType.MESH)

    loads = [pltpu.make_async_copy(src, dst, local.at[i]) for i, (src, dst) in enumerate(((x_in, x), (z_in, z), (tg_in, tg)))]
    for load in loads:
        load.start()

    t_i = lax.broadcasted_iota(jnp.int32, (tok, tok), 0)
    s_i = lax.broadcasted_iota(jnp.int32, (tok, tok), 1)
    diag, upto = t_i == s_i, s_i <= t_i

    def forms(row):
        wide = jnp.broadcast_to(row, (tok, tok))
        own = jnp.sum(jnp.where(diag, wide, 0.0), axis=1, keepdims=True)
        col = jnp.sum(jnp.where(upto, wide, 0.0), axis=1, keepdims=True)
        across = jnp.sum(jnp.where(t_i <= s_i, jnp.broadcast_to(own, (tok, tok)), 0.0), axis=0, keepdims=True)
        return own, col, across, jnp.sum(row, axis=1, keepdims=True)

    code_row = codes[...].astype(F32)
    code_own, cum_col, cum_row, cum_end = forms(code_row)
    _, seg_col, seg_row, seg_end = forms(segs[...].astype(F32))
    visible = upto & (seg_col == seg_row)
    c_mat, b_mat = ck[...], bk[...]
    dt_row = code_row * (1.0 / 64.0)
    gap = jnp.where(visible, (cum_col - cum_row) * (1.0 / 64.0), 0.0)
    dt_vis = jnp.where(visible, jnp.broadcast_to(dt_row, (tok, tok)), 0.0)
    cb_dt = mm_nt(c_mat, b_mat) * dt_vis
    tab[0], tab[1], tab[2], tab[3] = gap, cb_dt, cb_dt * gap, dt_vis
    shape = (tok, LANES)
    cols[0] = jnp.broadcast_to(cum_col * (1.0 / 64.0), shape)
    cols[1] = jnp.broadcast_to((cum_end - cum_col) * (1.0 / 64.0), shape)
    cols[2] = jnp.broadcast_to(jnp.where(seg_col == seg_end, code_own * (1.0 / 64.0), 0.0), shape)
    cols[3] = jnp.broadcast_to((seg_col == 0.0).astype(F32), shape)
    bt[...], ct[...] = b_mat.astype(F32).T.astype(BF16), c_mat.astype(F32).T.astype(BF16)
    end_dt = jnp.broadcast_to(cum_end * (1.0 / 64.0), (1, LANES))
    broken = jnp.broadcast_to((seg_end > 0.0).astype(F32), (1, LANES))
    meta[10] = jnp.where(
        lax.broadcasted_iota(jnp.int32, (8, LANES), 0) == 0, end_dt,
        jnp.where(lax.broadcasted_iota(jnp.int32, (8, LANES), 0) == 1, broken, 0.0),
    )
    acc[...] = jnp.zeros_like(acc)

    low = lax.broadcasted_iota(jnp.int32, (1, LANES), 1) < LANES // 2

    def rates(b):
        a0 = jnp.exp(jnp.full((1, LANES), lr[2 * b], F32))
        a1 = jnp.exp(jnp.full((1, LANES), lr[2 * b + 1], F32))
        return a0, a1, jnp.where(low, a0, a1)

    def skip_row(b):
        return jnp.where(low, jnp.full((1, LANES), sk[2 * b], F32), jnp.full((1, LANES), sk[2 * b + 1], F32))

    def decay_of(m, a):
        return jnp.where(m[1:2] > 0.0, 0.0, jnp.exp(-a * m[0:1]))

    def lanes(b):
        return pl.ds(pl.multiple_of(b * LANES, LANES), LANES)

    def pair(b):
        xb = x[:, lanes(b)]
        zero = jnp.zeros_like(xb)
        return jnp.concatenate([jnp.where(low, xb, zero), jnp.where(low, zero, xb)], axis=0)

    part = tok // SPLIT

    class Stage:
        def __init__(self, buf, sems, axis):
            self.buf, self.ss, self.rs = buf, sems[0], sems[1]
            self.mine, self.n, self.at = ((zi, zr, z_at), (xi, xr, x_at), (dpi, dpn, d_at))[axis]

        def hop(self, k, slot):
            return pltpu.make_async_remote_copy(
                src_ref=self.buf.at[slot], dst_ref=self.buf.at[slot], send_sem=self.ss.at[k], recv_sem=self.rs.at[k],
                device_id=self.at(k), device_id_type=pl.DeviceIdType.MESH,
            )

        def start(self, total):
            self.buf[self.mine] = total
            for k in range(1, self.n):
                self.hop(k, self.mine).start()

        def result(self):
            for k in range(1, self.n):
                self.hop(k, lax.rem(self.mine + self.n - k, self.n)).wait_recv()
            total = self.buf[0]
            for k in range(1, self.n):
                total = total + self.buf[k]
            return total

        def close(self):
            for k in range(1, self.n):
                self.hop(k, self.mine).wait_send()

    half, mid = nb // 2, zr // 2
    ticks = lambda hops: lax.div(hops * HOP[0], HOP[1])

    class Pass:
        def __init__(self, backward, out, recv, carry, partial):
            self.p = zr - 1 - zi if backward else zi
            self.r = xr - 1 - xi if backward else xi
            self.up, self.down = (z_at(zr - 1), z_at(1)) if backward else (z_at(1), z_at(zr - 1))
            self.across = x_at(xr - 1) if backward else x_at(1)
            self.out, self.recv, self.carry, self.part = out, recv, carry, partial
            self.base, self.backward = 5 * backward, backward
            self.sems = recv_sems[3 * backward : 3 * backward + 3]
            p, r = self.p, self.r
            self.low, self.high = p < mid, p >= mid
            self.first = [
                ticks(jnp.where(p < mid, p, zr - 1 - p)),
                ticks(jnp.where(p < mid, mid - 1 - p, p - mid)),
            ]
            self.second = [
                ticks(jnp.where(p < mid, jnp.where(r > 0, zr + r - p, p), r + p)),
                ticks(jnp.where(p < mid, mid + r + p, mid + r + zr - p)),
            ]

        def place_meta(self):
            slots = range(zr)
            at = lambda slot: zr - 1 - slot if self.backward else slot
            same = lambda q: self.low if q < mid else self.high
            rules = (
                lambda q: same(q) & (q < self.p),
                lambda q: same(q) & (q > self.p),
                lambda q: q < mid,
                lambda q: q >= mid,
                lambda q: True,
            )
            for n, rule in enumerate(rules):
                total = jnp.zeros((8, LANES), F32)
                for slot in slots:
                    total = total + jnp.where(rule(at(slot)), 1.0, 0.0) * row_meta[slot]
                meta[self.base + n] = total

        def decay(self, n, b):
            return decay_of(meta[self.base + n], rates(b)[2])

        def own(self, b):
            return decay_of(meta[10], rates(b)[2])

        def copy(self, src, dst, b, q, send, kind, to):
            cut = (b, pl.ds(q * part, part))
            return pltpu.make_async_remote_copy(
                src_ref=src.at[cut], dst_ref=dst.at[cut], send_sem=sends.at[send],
                recv_sem=self.sems[kind].at[b * SPLIT + q], device_id=to, device_id_type=pl.DeviceIdType.MESH,
            )

        def moves(self, s, b, q):
            sem = 6 * self.backward + 3 * s
            out, recv, carry, partial = self.out, self.recv, self.carry, self.part
            wait_recv = lambda: self.copy(recv, recv, b, q, sem, 0, self.up).wait_recv()
            wait_carry = lambda: self.copy(carry, carry, b, q, sem, 1, self.up).wait_recv()
            wait_part = lambda: self.copy(partial, partial, b, q, sem, 2, self.up).wait_recv()
            send_up = lambda: self.copy(out, recv, b, q, sem, 0, self.up).start()
            carry_down = lambda: self.copy(carry, carry, b, q, sem + 1, 1, self.down).start()
            part_down = lambda: self.copy(partial, partial, b, q, sem + 2, 2, self.down).start()
            return wait_recv, wait_carry, wait_part, send_up, carry_down, part_down

        def pieces(self, s, b, body):
            for q in range(SPLIT):
                body((b, pl.ds(q * part, part)), *self.moves(s, b, q))

        def scan_up(self, s, b):
            g = self.own(b)

            def body(cut, wait_recv, _, __, send_up, *___):
                wait_recv()
                self.out[cut] = self.out[cut] + g * self.recv[cut]
                send_up()

            self.pieces(s, b, body)

        def begin_up(self, s, b):
            self.pieces(s, b, lambda cut, _, __, ___, send_up, *____: send_up())
            self.recv[b] = jnp.zeros((tok, LANES), F32)

        def reduce_down(self, s, b, send):
            above = self.decay(1, b)

            def body(cut, _, __, wait_part, ___, ____, part_down):
                wait_part()
                self.part[cut] = self.part[cut] + above * self.out[cut]
                if send:
                    part_down()

            self.pieces(s, b, body)

        def begin_down(self, s, b):
            self.part[b] = self.out[b]
            self.pieces(s, b, lambda cut, _, __, ___, ____, _____, part_down: part_down())

        def spread(self, s, b, send):
            below = self.decay(0, b)

            def body(cut, _, wait_carry, __, ___, carry_down, ____):
                wait_carry()
                if send:
                    carry_down()
                self.recv[cut] = self.recv[cut] + below * self.carry[cut]

            self.pieces(s, b, body)

        def arrive(self, s, b):
            self.pieces(s, b, lambda cut, wait_recv, *_: wait_recv())

        def middle_first(self, b):
            p, r = self.p, self.r
            some = r < xr - 1
            for when, act in (
                ((p > 0) & (p < mid), lambda: self.scan_up(0, b)),
                (p == 0, lambda: self.begin_up(0, b)),
                ((p > mid) & (p < zr - 1) & some, lambda: self.reduce_down(0, b, True)),
                ((p == zr - 1) & some, lambda: self.begin_down(0, b)),
            ):
                pl.when(when)(act)

        def ends_first(self, b):
            p, r = self.p, self.r

            def at_end():
                g = self.own(b)
                for q in range(SPLIT):
                    cut = (b, pl.ds(q * part, part))
                    self.moves(1, b, q)[0]()
                    self.out[cut] = self.out[cut] + g * self.recv[cut]

                    @pl.when(r < xr - 1)
                    def _():
                        self.copy(self.out, self.carry, b, q, 6 * self.backward + 3, 1, self.up).start()

            for when, act in (
                ((p > 0) & (p < mid - 1), lambda: self.reduce_down(1, b, True)),
                (p == 0, lambda: self.reduce_down(1, b, False)),
                (p == mid - 1, lambda: self.begin_down(1, b)),
                (p == mid, lambda: self.begin_up(1, b)),
                ((p > mid) & (p < zr - 1), lambda: self.scan_up(1, b)),
                (p == zr - 1, at_end),
            ):
                pl.when(when)(act)

        def middle_second(self, b):
            p, r = self.p, self.r

            def root():
                g, above, low, high, row = self.own(b), *(self.decay(n, b) for n in (1, 2, 3, 4))
                for q in range(SPLIT):
                    cut = (b, pl.ds(q * part, part))
                    wait_recv, wait_carry, wait_part, send_up, carry_down, _ = self.moves(0, b, q)
                    wait_recv()

                    @pl.when(r < xr - 1)
                    def _():
                        wait_part()
                        self.part[cut] = self.part[cut] + above * self.out[cut] + high * self.recv[cut]

                    @pl.when(r > 0)
                    def _():
                        wait_carry()
                        carry_down()

                    @pl.when((r > 0) & (r < xr - 1))
                    def _():
                        self.part[cut] = self.part[cut] + row * self.carry[cut]

                    @pl.when(r < xr - 1)
                    def _():
                        self.copy(self.part, self.carry, b, q, 6 * self.backward + 2, 1, self.across).start()

                    @pl.when(r > 0)
                    def _():
                        self.recv[cut] = self.recv[cut] + low * self.carry[cut]

                    self.out[cut] = self.out[cut] + g * self.recv[cut]
                    send_up()

            for when, act in (
                ((p > 0) & (p < mid) & (r > 0), lambda: self.spread(0, b, True)),
                ((p == 0) & (r > 0), lambda: self.spread(0, b, False)),
                (p == mid, root),
                ((p > mid) & (p < zr - 1), lambda: self.scan_up(0, b)),
                (p == zr - 1, lambda: self.arrive(0, b)),
            ):
                pl.when(when)(act)

        def ends_second(self, b):
            p, r = self.p, self.r

            def root():
                g, low, high, row = self.own(b), *(self.decay(n, b) for n in (2, 3, 4))
                for q in range(SPLIT):
                    cut = (b, pl.ds(q * part, part))
                    wait_recv, wait_carry, _, send_up, *_ = self.moves(1, b, q)

                    @pl.when(r > 0)
                    def _():
                        wait_recv()

                    @pl.when(r == 0)
                    def _():
                        self.recv[cut] = jnp.zeros((part, LANES), F32)

                    @pl.when(r < xr - 1)
                    def _():
                        wait_carry()
                        self.carry[cut] = self.carry[cut] + high * self.part[cut] + row * self.recv[cut]
                        self.copy(self.carry, self.recv, b, q, 6 * self.backward + 4, 0, self.across).start()

                    self.out[cut] = self.out[cut] + g * self.recv[cut]
                    send_up()
                    self.part[cut] = self.part[cut] + low * self.recv[cut]
                    self.copy(self.part, self.carry, b, q, 6 * self.backward + 5, 1, self.down).start()

            for when, act in (
                (p == 0, root),
                ((p > 0) & (p < mid - 1), lambda: self.scan_up(1, b)),
                (p == mid - 1, lambda: self.arrive(1, b)),
                (p == mid, lambda: self.spread(1, b, False)),
                (p > mid, lambda: self.spread(1, b, True)),
            ):
                pl.when(when)(act)

        def finish(self):
            p, r = self.p, self.r
            sent = (
                (p < zr - 1),
                (p <= mid) & (p > 0) & (r > 0),
                (p >= mid) & (r < xr - 1),
                (p != mid - 1) & ((p < zr - 1) | (r < xr - 1)),
                ((p == 0) & (r < xr - 1)) | (p > mid),
                (p < mid),
            )
            for n, did in enumerate(sent):
                src = (self.out, self.carry, self.part)[n % 3].at[pl.ds(n // 3 * half, half)]
                move = pltpu.make_async_remote_copy(
                    src_ref=src, dst_ref=src, send_sem=sends.at[6 * self.backward + n], recv_sem=self.sems[0].at[0],
                    device_id=self.up, device_id_type=pl.DeviceIdType.MESH,
                )

                @pl.when(did)
                def _():
                    move.wait_send()

        def run(self, make, beside, then, events):
            def tick(i, _):
                def early(s, _):
                    c = i - jnp.where(s == 0, self.first[0], self.first[1])

                    @pl.when((c >= 0) & (c < half))
                    def _():
                        b = s * half + c
                        make(b)

                        @pl.when(s == 0)
                        def _():
                            self.middle_first(b)

                        @pl.when(s == 1)
                        def _():
                            self.ends_first(b)

                        beside(b)

                    return 0

                def late(s, _):
                    c = i - jnp.where(s == 0, self.second[0], self.second[1])

                    @pl.when((c >= 0) & (c < half))
                    def _():
                        b = s * half + c

                        @pl.when(s == 0)
                        def _():
                            self.middle_second(b)

                        @pl.when(s == 1)
                        def _():
                            self.ends_second(b)

                        then(b)

                    return 0

                lax.fori_loop(0, 2, early, 0)
                for when, event in events:
                    @pl.when(i == when)
                    def _():
                        event()

                lax.fori_loop(0, 2, late, 0)
                return 0

            lax.fori_loop(0, half + jnp.maximum(self.second[0], self.second[1]), tick, 0)

    fwd = Pass(False, f_out, p_st, f_carry, f_part)
    bwd = Pass(True, b_out, r_st, b_carry, b_part)
    meta_stage = Stage(row_meta, meta_sems, 0)

    def take_meta():
        meta_stage.result()
        fwd.place_meta()
        bwd.place_meta()

    def block_state(b):
        _, _, a = rates(b)
        u = (x[:, lanes(b)].astype(F32) * (jnp.exp(-a * cols[1]) * cols[2])).astype(BF16)
        ub[:, lanes(b)] = u
        f_out[b] = mm(bt[...], u)

    def scores_of(b):
        a0, a1, _ = rates(b)
        gap, cbd = tab[0], tab[1]
        e0, e1 = jnp.exp(-a0 * gap), jnp.exp(-a1 * gap)
        both = jnp.concatenate([(cbd * e0).astype(BF16), (cbd * e1).astype(BF16)], axis=1)
        return e0, e1, both

    def inside(b):
        _, _, both = scores_of(b)
        mix[:, lanes(b)] = mm(both, pair(b)) + skip_row(b) * x[:, lanes(b)].astype(F32)

    def mixture(b):
        _, _, a = rates(b)
        at = lanes(b)
        state = p_st[b].astype(BF16)
        inter[b] = state
        e = mm(c_mat_ref[...], state)
        ebuf[:, at] = e
        m = mix[:, at] + jnp.exp(-a * cols[0]) * cols[3] * e
        mix[:, at] = m
        zf = z[:, at].astype(F32)
        gated = m * (zf / (1.0 + jnp.exp(-zf)))
        gg = gated * gains[:, at]
        acc[0] += gated * gated
        acc[1] += gg * gg
        acc[2] += gg * tg[:, at].astype(F32)

    c_mat_ref, b_mat_ref = ck, bk

    pl.semaphore_wait(barrier, len(peers))
    meta_stage.start(meta[10])
    for load in loads:
        load.wait()
    fwd.run(block_state, inside, mixture, [(2, take_meta)])

    squares = jnp.sum(acc[0], axis=1, keepdims=True)
    r_col = lax.rsqrt(squares * (1.0 / width) + 1e-5)
    coef = r_col * r_col * r_col * (1.0 / width) * (
        r_col * jnp.sum(acc[1], axis=1, keepdims=True) - jnp.sum(acc[2], axis=1, keepdims=True)
    )
    cols[4] = jnp.broadcast_to(r_col, shape)
    cols[5] = jnp.broadcast_to(coef, shape)

    def direct(b):
        _, _, a = rates(b)
        at = lanes(b)
        m, xf, zf, gain, r = mix[:, at], x[:, at].astype(F32), z[:, at].astype(F32), gains[:, at], cols[4]
        sig = 1.0 / (1.0 + jnp.exp(-zf))
        sg = zf * sig
        gated = m * sg
        unit = gated * r
        miss = unit * gain - tg[:, at].astype(F32)
        dgated = r * (miss * gain) - gated * cols[5]
        dmix = dgated * sg
        de = jnp.exp(-a * cols[0]) * cols[3] * dmix
        deb = de.astype(BF16)
        b_out[b] = mm(ct[...], deb)
        mix[:, at] = dmix
        gz[:, at] = (dgated * m * (sig * (1.0 + zf * (1.0 - sig)))).astype(BF16)
        acc[3, 0:8] += red8(miss * miss)
        ga[b] = red8(miss * unit)
        sa[b] = red8(dmix * xf)
        ra[b] = red8(cols[0] * de * ebuf[:, at])
        acc[4] += mm_nt(deb, inter[b])

    def inside_back(b):
        at = lanes(b)
        e0, e1, both = scores_of(b)
        dmix = mix[:, at]
        dmb = dmix.astype(BF16)
        ds = mm_nt(dmb, pair(b))
        d0, d1 = ds[:, :tok] * e0, ds[:, tok:] * e1
        acc[5] += d0 + d1
        v0, v1 = red8(d0 * tab[2]), red8(d1 * tab[2])
        ra[b] += jnp.where(low, v0 + pltpu.roll(v0, LANES // 2, 1), v1 + pltpu.roll(v1, LANES // 2, 1))
        back = mm_tn(both, dmb)
        dxa[:, at] = jnp.where(low, back[:tok], back[tok:]) + skip_row(b) * dmix

    def state_back(b):
        _, _, a = rates(b)
        at = lanes(b)
        by = r_st[b]
        byb = by.astype(BF16)
        duw = mm(b_mat_ref[...], byb) * (jnp.exp(-a * cols[1]) * cols[2])
        gx[:, at] = (dxa[:, at] + duw).astype(BF16)
        own = meta[10]
        ra[b] += red8(cols[1] * duw * x[:, at].astype(F32)) + red8(by * p_st[b]) * (own[0:1] * decay_of(own, a))
        acc[6] += mm_nt(ub[:, at], byb)

    lane8 = lax.broadcasted_iota(jnp.int32, (8, LANES), 1)
    row8 = lax.broadcasted_iota(jnp.int32, (8, LANES), 0)

    def by_head(rows):
        h0 = jnp.sum(jnp.where(low, rows, 0.0), axis=1, keepdims=True)
        h1 = jnp.sum(jnp.where(low, 0.0, rows), axis=1, keepdims=True)
        tile = jnp.zeros((8, LANES), F32)
        for g in range(nb // 8):
            cut, lane = slice(8 * g, 8 * g + 8), 16 * g + 2 * row8
            tile += jnp.where(lane8 == lane, h0[cut], 0.0) + jnp.where(lane8 == lane + 1, h1[cut], 0.0)
        return tile

    w_stage = [Stage(wide_bufs[i], wide_sems[i], i) for i in range(3)]
    r_stage = [Stage(rate_bufs[i], rate_sems[i], i) for i in range(3)]

    store_gz = pltpu.make_async_copy(gz, gz_out, local.at[3])
    store_gx = pltpu.make_async_copy(gx, gx_out, local.at[4])

    def early_sums():
        store_gz.start()
        lost = 0.5 * jnp.sum(acc[3, 0:8], axis=1, keepdims=True)
        tile = by_head(sa[...].sum(axis=1)) + jnp.where(lane8 == LANES - 1, lost, 0.0)
        w_stage[0].start(jnp.concatenate([ga[...].sum(axis=1), tile], axis=0))

    def wide_across():
        w_stage[1].start(w_stage[0].result())

    end = half + jnp.maximum(bwd.second[0], bwd.second[1])
    made = half - 1 + jnp.maximum(bwd.first[0], bwd.first[1])
    bwd.run(direct, inside_back, state_back, [(made, early_sums), (jnp.where(bwd.r > 0, end - 4, end), wide_across)])
    store_gx.start()

    a_rows = jnp.concatenate([rates(b)[2] for b in range(nb)], axis=0)
    r_stage[0].start(by_head(ra[...].sum(axis=1) * -a_rows))

    @pl.when(bwd.r == 0)
    def _():
        wide_across()

    w_stage[2].start(w_stage[1].result())
    dcb = (acc[5] * tab[3]).astype(BF16)
    gc[...] = (acc[4] + mm(dcb, bk[...])).astype(BF16)
    gb[...] = (acc[6] + mm_tn(dcb, ck[...])).astype(BF16)
    r_stage[1].start(r_stage[0].result())
    r_stage[2].start(r_stage[1].result())
    red[...] = w_stage[2].result() * (1.0 / rows_total)
    fwd.finish()
    bwd.finish()
    meta_stage.close()
    for stage in w_stage + r_stage[:2]:
        stage.close()
    store_gz.wait()
    store_gx.wait()
    red_rates[...] = r_stage[2].result() * (1.0 / rows_total)
    r_stage[2].close()


def hand_over(nb, gx, gz, gb, gc, red, red_rates, gx_out, gz_out, gb_out, gc_out, loss, rate, skip, gain, stage, sems):
    rows = gx.shape[0] // PIECES
    moves = []
    for i, (src, dst) in enumerate(((gx, gx_out), (gz, gz_out))):
        for j in range(PIECES):
            cut, n = pl.ds(j * rows, rows), i * PIECES + j
            moves.append((
                pltpu.make_async_copy(src.at[cut], stage.at[i, cut], sems.at[0, n]),
                pltpu.make_async_copy(stage.at[i, cut], dst.at[cut], sems.at[1, n]),
            ))
    for fetch, _ in moves:
        fetch.start()
    gb_out[...] = gb[...]
    gc_out[...] = gc[...]
    for b in range(nb):
        gain[:, b * LANES : (b + 1) * LANES] = red[b : b + 1, :]
    tail = jnp.sum(red[nb:, :], axis=0, keepdims=True)
    loss[...] = tail[:, LANES - 1 :]
    skip[...] = tail[:, : 2 * nb]
    rate[...] = jnp.sum(red_rates[...], axis=0, keepdims=True)[:, : 2 * nb]
    for fetch, store in moves:
        fetch.wait()
        store.start()
    for _, store in moves:
        store.wait()


def shards(mesh, inputs, gates, keys_b, reads_c, step_codes, seg_starts, targets, log_rates, skips, gains):
    tok, width = inputs.shape[1:]
    nb = width // LANES
    seq, dpn = mesh.shape["seq"], mesh.shape["dp"]
    zr = min(Z_RING, seq)
    xr = seq // zr
    vmem, smem = pl.BlockSpec(memory_space=pltpu.VMEM), pl.BlockSpec(memory_space=pltpu.SMEM)
    hbm = pl.BlockSpec(memory_space=pltpu.HBM)
    rows = nb + 8
    state = pltpu.VMEM((nb, tok, LANES), F32)
    dma = pltpu.SemaphoreType.DMA
    counts = (zr, xr, dpn)
    of = jax.ShapeDtypeStruct
    wide, small = of((tok, width), BF16), of(keys_b.shape[1:], BF16)
    flat, half = pltpu.VMEM((tok, width), F32), pltpu.VMEM((tok, width), BF16)
    results = pl.pallas_call(
        functools.partial(kernel, xr, zr, dpn, nb, float(tok * seq * dpn)),
        out_shape=(wide, wide, small, small, of((rows, LANES), F32), of((8, LANES), F32)),
        in_specs=[smem] * 2 + [hbm] * 3 + [vmem] * 5,
        out_specs=(hbm,) * 2 + (vmem,) * 4,
        scratch_shapes=[half] * 5
        + [state] * 8
        + [
            flat,
            flat,
            flat,
            pltpu.VMEM((nb, tok, LANES), BF16),
            half,
            pltpu.VMEM((6, tok, LANES), F32),
            pltpu.VMEM((4, tok, tok), F32),
            pltpu.VMEM((7, tok, LANES), F32),
            pltpu.VMEM((nb, 8, LANES), F32),
            pltpu.VMEM((nb, 8, LANES), F32),
            pltpu.VMEM((nb, 8, LANES), F32),
            pltpu.VMEM((LANES, tok), BF16),
            pltpu.VMEM((LANES, tok), BF16),
            pltpu.VMEM((11, 8, LANES), F32),
            pltpu.VMEM((zr, 8, LANES), F32),
            [pltpu.VMEM((n, rows, LANES), F32) for n in counts],
            [pltpu.VMEM((n, 8, LANES), F32) for n in counts],
        ]
        + [[dma((nb * SPLIT,))] * 6, dma((12,)), dma((5,))]
        + [[[dma((n,)), dma((n,))] for n in counts] for _ in range(2)]
        + [[dma((zr,)), dma((zr,))]],
        compiler_params=pltpu.CompilerParams(
            collective_id=0, has_side_effects=True, vmem_limit_bytes=56 * 1024 * 1024
        ),
        name="mixer",
    )(
        log_rates, skips, inputs[0], gates[0], targets[0], keys_b[0], reads_c[0],
        step_codes, seg_starts, gains.reshape(1, width),
    )
    line = of((1, 2 * nb), F32)
    gx, gz, gb, gc, loss, rate, skip, gain = pl.pallas_call(
        functools.partial(hand_over, nb),
        out_shape=(wide, wide, small, small, of((1, 1), F32), line, line, of((1, width), F32)),
        in_specs=[hbm] * 2 + [vmem] * 4,
        out_specs=(hbm,) * 2 + (vmem,) * 6,
        scratch_shapes=[pltpu.VMEM((2, tok, width), BF16), dma((2, 2 * PIECES))],
        name="hand_over",
    )(*results)
    return (
        loss[0, 0], gx[None], gz[None], gb[None], gc[None], rate[0], skip[0], gain[0],
    )


def solution(mesh):
    wide, line = P("dp", "seq", None), P("dp", "seq")
    return jax.shard_map(
        functools.partial(shards, mesh),
        mesh=mesh,
        in_specs=(wide, wide, wide, wide, line, line, wide, P(), P(), P()),
        out_specs=(P(), wide, wide, wide, wide, P(), P(), P()),
        check_vma=False,
    )
```

```python
import functools

import jax
import jax.numpy as jnp
from jax import lax
from jax.experimental import pallas as pl
from jax.experimental.pallas import tpu as pltpu
from jax.sharding import PartitionSpec as P

F32, BF16 = jnp.float32, jnp.bfloat16
LANES = 128
Z_RING = 8
SPLIT = 2
HOP = (26, 8)
PIECES = 4


def red8(v):
    return v.reshape(v.shape[0] // 8, 8, LANES).sum(axis=0)


def mm(a, b):
    return lax.dot_general(a, b, (((1,), (0,)), ((), ())), preferred_element_type=F32)


def mm_nt(a, b):
    return lax.dot_general(a, b, (((1,), (1,)), ((), ())), preferred_element_type=F32)


def mm_tn(a, b):
    return lax.dot_general(a, b, (((0,), (0,)), ((), ())), preferred_element_type=F32)


def kernel(
    xr, zr, dpn, nb, rows_total,
    lr, sk, x_in, z_in, tg_in, bk, ck, codes, segs, gains,
    gx_out, gz_out, gb, gc, red, red_rates,
    x, z, tg, gx, gz,
    f_out, p_st, f_carry, f_part, b_out, r_st, b_carry, b_part,
    mix, ebuf, dxa, inter, ub,
    cols, tab, acc, ga, sa, ra, bt, ct, meta, row_meta,
    wide_bufs, rate_bufs,
    recv_sems, sends, local,
    wide_sems, rate_sems, meta_sems,
):
    tok = x.shape[0]
    width = nb * LANES
    me, dpi = lax.axis_index("seq"), lax.axis_index("dp")
    zi, xi = lax.rem(me, zr), lax.div(me, zr)
    z_at = lambda k: {"seq": xi * zr + lax.rem(zi + k, zr)}
    x_at = lambda k: {"seq": lax.rem(xi + k, xr) * zr + zi}
    d_at = lambda k: {"dp": lax.rem(dpi + k, dpn)}

    barrier = pltpu.get_barrier_semaphore()
    peers = [z_at(k) for k in range(1, zr)] + [x_at(k) for k in range(1, xr)] + [d_at(k) for k in range(1, dpn)]
    for peer in peers:
        pl.semaphore_signal(barrier, inc=1, device_id=peer, device_id_type=pl.DeviceIdType.MESH)

    loads = [pltpu.make_async_copy(src, dst, local.at[i]) for i, (src, dst) in enumerate(((x_in, x), (z_in, z), (tg_in, tg)))]
    for load in loads:
        load.start()

    t_i = lax.broadcasted_iota(jnp.int32, (tok, tok), 0)
    s_i = lax.broadcasted_iota(jnp.int32, (tok, tok), 1)
    diag, upto = t_i == s_i, s_i <= t_i

    def forms(row):
        wide = jnp.broadcast_to(row, (tok, tok))
        own = jnp.sum(jnp.where(diag, wide, 0.0), axis=1, keepdims=True)
        col = jnp.sum(jnp.where(upto, wide, 0.0), axis=1, keepdims=True)
        across = jnp.sum(jnp.where(t_i <= s_i, jnp.broadcast_to(own, (tok, tok)), 0.0), axis=0, keepdims=True)
        return own, col, across, jnp.sum(row, axis=1, keepdims=True)

    code_row = codes[...].astype(F32)
    code_own, cum_col, cum_row, cum_end = forms(code_row)
    _, seg_col, seg_row, seg_end = forms(segs[...].astype(F32))
    visible = upto & (seg_col == seg_row)
    c_mat, b_mat = ck[...], bk[...]
    dt_row = code_row * (1.0 / 64.0)
    gap = jnp.where(visible, (cum_col - cum_row) * (1.0 / 64.0), 0.0)
    dt_vis = jnp.where(visible, jnp.broadcast_to(dt_row, (tok, tok)), 0.0)
    cb_dt = mm_nt(c_mat, b_mat) * dt_vis
    tab[0], tab[1], tab[2], tab[3] = gap, cb_dt, cb_dt * gap, dt_vis
    shape = (tok, LANES)
    cols[0] = jnp.broadcast_to(cum_col * (1.0 / 64.0), shape)
    cols[1] = jnp.broadcast_to((cum_end - cum_col) * (1.0 / 64.0), shape)
    cols[2] = jnp.broadcast_to(jnp.where(seg_col == seg_end, code_own * (1.0 / 64.0), 0.0), shape)
    cols[3] = jnp.broadcast_to((seg_col == 0.0).astype(F32), shape)
    bt[...], ct[...] = b_mat.astype(F32).T.astype(BF16), c_mat.astype(F32).T.astype(BF16)
    end_dt = jnp.broadcast_to(cum_end * (1.0 / 64.0), (1, LANES))
    broken = jnp.broadcast_to((seg_end > 0.0).astype(F32), (1, LANES))
    meta[10] = jnp.where(
        lax.broadcasted_iota(jnp.int32, (8, LANES), 0) == 0, end_dt,
        jnp.where(lax.broadcasted_iota(jnp.int32, (8, LANES), 0) == 1, broken, 0.0),
    )
    acc[...] = jnp.zeros_like(acc)

    low = lax.broadcasted_iota(jnp.int32, (1, LANES), 1) < LANES // 2

    def rates(b):
        a0 = jnp.exp(jnp.full((1, LANES), lr[2 * b], F32))
        a1 = jnp.exp(jnp.full((1, LANES), lr[2 * b + 1], F32))
        return a0, a1, jnp.where(low, a0, a1)

    def skip_row(b):
        return jnp.where(low, jnp.full((1, LANES), sk[2 * b], F32), jnp.full((1, LANES), sk[2 * b + 1], F32))

    def decay_of(m, a):
        return jnp.where(m[1:2] > 0.0, 0.0, jnp.exp(-a * m[0:1]))

    def lanes(b):
        return pl.ds(pl.multiple_of(b * LANES, LANES), LANES)

    def pair(b):
        xb = x[:, lanes(b)]
        zero = jnp.zeros_like(xb)
        return jnp.concatenate([jnp.where(low, xb, zero), jnp.where(low, zero, xb)], axis=0)

    part = tok // SPLIT

    class Stage:
        def __init__(self, buf, sems, axis):
            self.buf, self.ss, self.rs = buf, sems[0], sems[1]
            self.mine, self.n, self.at = ((zi, zr, z_at), (xi, xr, x_at), (dpi, dpn, d_at))[axis]

        def hop(self, k, slot):
            return pltpu.make_async_remote_copy(
                src_ref=self.buf.at[slot], dst_ref=self.buf.at[slot], send_sem=self.ss.at[k], recv_sem=self.rs.at[k],
                device_id=self.at(k), device_id_type=pl.DeviceIdType.MESH,
            )

        def start(self, total):
            self.buf[self.mine] = total
            for k in range(1, self.n):
                self.hop(k, self.mine).start()

        def result(self):
            for k in range(1, self.n):
                self.hop(k, lax.rem(self.mine + self.n - k, self.n)).wait_recv()
            total = self.buf[0]
            for k in range(1, self.n):
                total = total + self.buf[k]
            return total

        def close(self):
            for k in range(1, self.n):
                self.hop(k, self.mine).wait_send()

    half, mid = nb // 2, zr // 2
    ticks = lambda hops: lax.div(hops * HOP[0], HOP[1])

    class Pass:
        def __init__(self, backward, out, recv, carry, partial):
            self.p = zr - 1 - zi if backward else zi
            self.r = xr - 1 - xi if backward else xi
            self.up, self.down = (z_at(zr - 1), z_at(1)) if backward else (z_at(1), z_at(zr - 1))
            self.across = x_at(xr - 1) if backward else x_at(1)
            self.out, self.recv, self.carry, self.part = out, recv, carry, partial
            self.base, self.backward = 5 * backward, backward
            self.sems = recv_sems[3 * backward : 3 * backward + 3]
            p, r = self.p, self.r
            self.low, self.high = p < mid, p >= mid
            self.first = [
                ticks(jnp.where(p < mid, p, zr - 1 - p)),
                ticks(jnp.where(p < mid, mid - 1 - p, p - mid)),
            ]
            self.second = [
                ticks(jnp.where(p < mid, jnp.where(r > 0, zr + r - p, p), r + p)),
                ticks(jnp.where(p < mid, mid + r + p, mid + r + zr - p)),
            ]

        def place_meta(self):
            slots = range(zr)
            at = lambda slot: zr - 1 - slot if self.backward else slot
            same = lambda q: self.low if q < mid else self.high
            rules = (
                lambda q: same(q) & (q < self.p),
                lambda q: same(q) & (q > self.p),
                lambda q: q < mid,
                lambda q: q >= mid,
                lambda q: True,
            )
            for n, rule in enumerate(rules):
                total = jnp.zeros((8, LANES), F32)
                for slot in slots:
                    total = total + jnp.where(rule(at(slot)), 1.0, 0.0) * row_meta[slot]
                meta[self.base + n] = total

        def decay(self, n, b):
            return decay_of(meta[self.base + n], rates(b)[2])

        def own(self, b):
            return decay_of(meta[10], rates(b)[2])

        def copy(self, src, dst, b, q, send, kind, to):
            cut = (b, pl.ds(q * part, part))
            return pltpu.make_async_remote_copy(
                src_ref=src.at[cut], dst_ref=dst.at[cut], send_sem=sends.at[send],
                recv_sem=self.sems[kind].at[b * SPLIT + q], device_id=to, device_id_type=pl.DeviceIdType.MESH,
            )

        def moves(self, s, b, q):
            sem = 6 * self.backward + 3 * s
            out, recv, carry, partial = self.out, self.recv, self.carry, self.part
            wait_recv = lambda: self.copy(recv, recv, b, q, sem, 0, self.up).wait_recv()
            wait_carry = lambda: self.copy(carry, carry, b, q, sem, 1, self.up).wait_recv()
            wait_part = lambda: self.copy(partial, partial, b, q, sem, 2, self.up).wait_recv()
            send_up = lambda: self.copy(out, recv, b, q, sem, 0, self.up).start()
            carry_down = lambda: self.copy(carry, carry, b, q, sem + 1, 1, self.down).start()
            part_down = lambda: self.copy(partial, partial, b, q, sem + 2, 2, self.down).start()
            return wait_recv, wait_carry, wait_part, send_up, carry_down, part_down

        def pieces(self, s, b, body):
            for q in range(SPLIT):
                body((b, pl.ds(q * part, part)), *self.moves(s, b, q))

        def scan_up(self, s, b):
            g = self.own(b)

            def body(cut, wait_recv, _, __, send_up, *___):
                wait_recv()
                self.out[cut] = self.out[cut] + g * self.recv[cut]
                send_up()

            self.pieces(s, b, body)

        def begin_up(self, s, b):
            self.pieces(s, b, lambda cut, _, __, ___, send_up, *____: send_up())
            self.recv[b] = jnp.zeros((tok, LANES), F32)

        def reduce_down(self, s, b, send):
            above = self.decay(1, b)

            def body(cut, _, __, wait_part, ___, ____, part_down):
                wait_part()
                self.part[cut] = self.part[cut] + above * self.out[cut]
                if send:
                    part_down()

            self.pieces(s, b, body)

        def begin_down(self, s, b):
            self.part[b] = self.out[b]
            self.pieces(s, b, lambda cut, _, __, ___, ____, _____, part_down: part_down())

        def spread(self, s, b, send):
            below = self.decay(0, b)

            def body(cut, _, wait_carry, __, ___, carry_down, ____):
                wait_carry()
                if send:
                    carry_down()
                self.recv[cut] = self.recv[cut] + below * self.carry[cut]

            self.pieces(s, b, body)

        def arrive(self, s, b):
            self.pieces(s, b, lambda cut, wait_recv, *_: wait_recv())

        def middle_first(self, b):
            p, r = self.p, self.r
            some = r < xr - 1
            for when, act in (
                ((p > 0) & (p < mid), lambda: self.scan_up(0, b)),
                (p == 0, lambda: self.begin_up(0, b)),
                ((p > mid) & (p < zr - 1) & some, lambda: self.reduce_down(0, b, True)),
                ((p == zr - 1) & some, lambda: self.begin_down(0, b)),
            ):
                pl.when(when)(act)

        def ends_first(self, b):
            p, r = self.p, self.r

            def at_end():
                g = self.own(b)
                for q in range(SPLIT):
                    cut = (b, pl.ds(q * part, part))
                    self.moves(1, b, q)[0]()
                    self.out[cut] = self.out[cut] + g * self.recv[cut]

                    @pl.when(r < xr - 1)
                    def _():
                        self.copy(self.out, self.carry, b, q, 6 * self.backward + 3, 1, self.up).start()

            for when, act in (
                ((p > 0) & (p < mid - 1), lambda: self.reduce_down(1, b, True)),
                (p == 0, lambda: self.reduce_down(1, b, False)),
                (p == mid - 1, lambda: self.begin_down(1, b)),
                (p == mid, lambda: self.begin_up(1, b)),
                ((p > mid) & (p < zr - 1), lambda: self.scan_up(1, b)),
                (p == zr - 1, at_end),
            ):
                pl.when(when)(act)

        def middle_second(self, b):
            p, r = self.p, self.r

            def root():
                g, above, low, high, row = self.own(b), *(self.decay(n, b) for n in (1, 2, 3, 4))
                for q in range(SPLIT):
                    cut = (b, pl.ds(q * part, part))
                    wait_recv, wait_carry, wait_part, send_up, carry_down, _ = self.moves(0, b, q)
                    wait_recv()

                    @pl.when(r < xr - 1)
                    def _():
                        wait_part()
                        self.part[cut] = self.part[cut] + above * self.out[cut] + high * self.recv[cut]

                    @pl.when(r > 0)
                    def _():
                        wait_carry()
                        carry_down()

                    @pl.when((r > 0) & (r < xr - 1))
                    def _():
                        self.part[cut] = self.part[cut] + row * self.carry[cut]

                    @pl.when(r < xr - 1)
                    def _():
                        self.copy(self.part, self.carry, b, q, 6 * self.backward + 2, 1, self.across).start()

                    @pl.when(r > 0)
                    def _():
                        self.recv[cut] = self.recv[cut] + low * self.carry[cut]

                    self.out[cut] = self.out[cut] + g * self.recv[cut]
                    send_up()

            for when, act in (
                ((p > 0) & (p < mid) & (r > 0), lambda: self.spread(0, b, True)),
                ((p == 0) & (r > 0), lambda: self.spread(0, b, False)),
                (p == mid, root),
                ((p > mid) & (p < zr - 1), lambda: self.scan_up(0, b)),
                (p == zr - 1, lambda: self.arrive(0, b)),
            ):
                pl.when(when)(act)

        def ends_second(self, b):
            p, r = self.p, self.r

            def root():
                g, low, high, row = self.own(b), *(self.decay(n, b) for n in (2, 3, 4))
                for q in range(SPLIT):
                    cut = (b, pl.ds(q * part, part))
                    wait_recv, wait_carry, _, send_up, *_ = self.moves(1, b, q)

                    @pl.when(r > 0)
                    def _():
                        wait_recv()

                    @pl.when(r == 0)
                    def _():
                        self.recv[cut] = jnp.zeros((part, LANES), F32)

                    @pl.when(r < xr - 1)
                    def _():
                        wait_carry()
                        self.carry[cut] = self.carry[cut] + high * self.part[cut] + row * self.recv[cut]
                        self.copy(self.carry, self.recv, b, q, 6 * self.backward + 4, 0, self.across).start()

                    self.out[cut] = self.out[cut] + g * self.recv[cut]
                    send_up()
                    self.part[cut] = self.part[cut] + low * self.recv[cut]
                    self.copy(self.part, self.carry, b, q, 6 * self.backward + 5, 1, self.down).start()

            for when, act in (
                (p == 0, root),
                ((p > 0) & (p < mid - 1), lambda: self.scan_up(1, b)),
                (p == mid - 1, lambda: self.arrive(1, b)),
                (p == mid, lambda: self.spread(1, b, False)),
                (p > mid, lambda: self.spread(1, b, True)),
            ):
                pl.when(when)(act)

        def finish(self):
            p, r = self.p, self.r
            sent = (
                (p < zr - 1),
                (p <= mid) & (p > 0) & (r > 0),
                (p >= mid) & (r < xr - 1),
                (p != mid - 1) & ((p < zr - 1) | (r < xr - 1)),
                ((p == 0) & (r < xr - 1)) | (p > mid),
                (p < mid),
            )
            for n, did in enumerate(sent):
                src = (self.out, self.carry, self.part)[n % 3].at[pl.ds(n // 3 * half, half)]
                move = pltpu.make_async_remote_copy(
                    src_ref=src, dst_ref=src, send_sem=sends.at[6 * self.backward + n], recv_sem=self.sems[0].at[0],
                    device_id=self.up, device_id_type=pl.DeviceIdType.MESH,
                )

                @pl.when(did)
                def _():
                    move.wait_send()

        def run(self, make, beside, then, events):
            def tick(i, _):
                def early(s, _):
                    c = i - jnp.where(s == 0, self.first[0], self.first[1])

                    @pl.when((c >= 0) & (c < half))
                    def _():
                        b = s * half + c
                        make(b)

                        @pl.when(s == 0)
                        def _():
                            self.middle_first(b)

                        @pl.when(s == 1)
                        def _():
                            self.ends_first(b)

                        beside(b)

                    return 0

                def late(s, _):
                    c = i - jnp.where(s == 0, self.second[0], self.second[1])

                    @pl.when((c >= 0) & (c < half))
                    def _():
                        b = s * half + c

                        @pl.when(s == 0)
                        def _():
                            self.middle_second(b)

                        @pl.when(s == 1)
                        def _():
                            self.ends_second(b)

                        then(b)

                    return 0

                lax.fori_loop(0, 2, early, 0)
                for when, event in events:
                    @pl.when(i == when)
                    def _():
                        event()

                lax.fori_loop(0, 2, late, 0)
                return 0

            lax.fori_loop(0, half + jnp.maximum(self.second[0], self.second[1]), tick, 0)

    fwd = Pass(False, f_out, p_st, f_carry, f_part)
    bwd = Pass(True, b_out, r_st, b_carry, b_part)
    meta_stage = Stage(row_meta, meta_sems, 0)

    def take_meta():
        meta_stage.result()
        fwd.place_meta()
        bwd.place_meta()

    def block_state(b):
        _, _, a = rates(b)
        u = (x[:, lanes(b)].astype(F32) * (jnp.exp(-a * cols[1]) * cols[2])).astype(BF16)
        ub[:, lanes(b)] = u
        f_out[b] = mm(bt[...], u)

    def scores_of(b):
        a0, a1, _ = rates(b)
        gap, cbd = tab[0], tab[1]
        e0, e1 = jnp.exp(-a0 * gap), jnp.exp(-a1 * gap)
        both = jnp.concatenate([(cbd * e0).astype(BF16), (cbd * e1).astype(BF16)], axis=1)
        return e0, e1, both

    def inside(b):
        _, _, both = scores_of(b)
        mix[:, lanes(b)] = mm(both, pair(b)) + skip_row(b) * x[:, lanes(b)].astype(F32)

    def mixture(b):
        _, _, a = rates(b)
        at = lanes(b)
        state = p_st[b].astype(BF16)
        inter[b] = state
        e = mm(c_mat_ref[...], state)
        ebuf[:, at] = e
        m = mix[:, at] + jnp.exp(-a * cols[0]) * cols[3] * e
        mix[:, at] = m
        zf = z[:, at].astype(F32)
        gated = m * (zf / (1.0 + jnp.exp(-zf)))
        gg = gated * gains[:, at]
        acc[0] += gated * gated
        acc[1] += gg * gg
        acc[2] += gg * tg[:, at].astype(F32)

    c_mat_ref, b_mat_ref = ck, bk

    pl.semaphore_wait(barrier, len(peers))
    meta_stage.start(meta[10])
    for load in loads:
        load.wait()
    fwd.run(block_state, inside, mixture, [(2, take_meta)])

    squares = jnp.sum(acc[0], axis=1, keepdims=True)
    r_col = lax.rsqrt(squares * (1.0 / width) + 1e-5)
    coef = r_col * r_col * r_col * (1.0 / width) * (
        r_col * jnp.sum(acc[1], axis=1, keepdims=True) - jnp.sum(acc[2], axis=1, keepdims=True)
    )
    cols[4] = jnp.broadcast_to(r_col, shape)
    cols[5] = jnp.broadcast_to(coef, shape)

    def direct(b):
        _, _, a = rates(b)
        at = lanes(b)
        m, xf, zf, gain, r = mix[:, at], x[:, at].astype(F32), z[:, at].astype(F32), gains[:, at], cols[4]
        sig = 1.0 / (1.0 + jnp.exp(-zf))
        sg = zf * sig
        gated = m * sg
        unit = gated * r
        miss = unit * gain - tg[:, at].astype(F32)
        dgated = r * (miss * gain) - gated * cols[5]
        dmix = dgated * sg
        de = jnp.exp(-a * cols[0]) * cols[3] * dmix
        deb = de.astype(BF16)
        b_out[b] = mm(ct[...], deb)
        mix[:, at] = dmix
        gz[:, at] = (dgated * m * (sig * (1.0 + zf * (1.0 - sig)))).astype(BF16)
        acc[3, 0:8] += red8(miss * miss)
        ga[b] = red8(miss * unit)
        sa[b] = red8(dmix * xf)
        ra[b] = red8(cols[0] * de * ebuf[:, at])
        acc[4] += mm_nt(deb, inter[b])

    def inside_back(b):
        at = lanes(b)
        e0, e1, both = scores_of(b)
        dmix = mix[:, at]
        dmb = dmix.astype(BF16)
        ds = mm_nt(dmb, pair(b))
        d0, d1 = ds[:, :tok] * e0, ds[:, tok:] * e1
        acc[5] += d0 + d1
        v0, v1 = red8(d0 * tab[2]), red8(d1 * tab[2])
        ra[b] += jnp.where(low, v0 + pltpu.roll(v0, LANES // 2, 1), v1 + pltpu.roll(v1, LANES // 2, 1))
        back = mm_tn(both, dmb)
        dxa[:, at] = jnp.where(low, back[:tok], back[tok:]) + skip_row(b) * dmix

    def state_back(b):
        _, _, a = rates(b)
        at = lanes(b)
        by = r_st[b]
        byb = by.astype(BF16)
        duw = mm(b_mat_ref[...], byb) * (jnp.exp(-a * cols[1]) * cols[2])
        gx[:, at] = (dxa[:, at] + duw).astype(BF16)
        own = meta[10]
        late = red8(cols[1] * duw * x[:, at].astype(F32)) + red8(by * p_st[b]) * (own[0:1] * decay_of(own, a))
        ra[b] = (ra[b] + late) * -a
        acc[6] += mm_nt(ub[:, at], byb)

    lane8 = lax.broadcasted_iota(jnp.int32, (8, LANES), 1)
    row8 = lax.broadcasted_iota(jnp.int32, (8, LANES), 0)

    def by_head(rows):
        h0 = jnp.sum(jnp.where(low, rows, 0.0), axis=1, keepdims=True)
        h1 = jnp.sum(jnp.where(low, 0.0, rows), axis=1, keepdims=True)
        tile = jnp.zeros((8, LANES), F32)
        for g in range(nb // 8):
            cut, lane = slice(8 * g, 8 * g + 8), 16 * g + 2 * row8
            tile += jnp.where(lane8 == lane, h0[cut], 0.0) + jnp.where(lane8 == lane + 1, h1[cut], 0.0)
        return tile

    w_stage = [Stage(wide_bufs[i], wide_sems[i], i) for i in range(3)]
    r_stage = [Stage(rate_bufs[i], rate_sems[i], i) for i in range(3)]

    store_gz = pltpu.make_async_copy(gz, gz_out, local.at[3])
    store_gx = pltpu.make_async_copy(gx, gx_out, local.at[4])

    def early_sums():
        store_gz.start()
        lost = 0.5 * jnp.sum(acc[3, 0:8], axis=1, keepdims=True)
        tile = by_head(sa[...].sum(axis=1)) + jnp.where(lane8 == LANES - 1, lost, 0.0)
        w_stage[0].start(jnp.concatenate([ga[...].sum(axis=1), tile], axis=0))

    def wide_across():
        w_stage[1].start(w_stage[0].result())

    end = half + jnp.maximum(bwd.second[0], bwd.second[1])
    made = half - 1 + jnp.maximum(bwd.first[0], bwd.first[1])
    bwd.run(direct, inside_back, state_back, [(made, early_sums), (jnp.where(bwd.r > 0, end - 4, end), wide_across)])
    store_gx.start()

    r_stage[0].start(by_head(ra[...].sum(axis=1)))

    @pl.when(bwd.r == 0)
    def _():
        wide_across()

    w_stage[2].start(w_stage[1].result())
    dcb = (acc[5] * tab[3]).astype(BF16)
    gc[...] = (acc[4] + mm(dcb, bk[...])).astype(BF16)
    gb[...] = (acc[6] + mm_tn(dcb, ck[...])).astype(BF16)
    r_stage[1].start(r_stage[0].result())
    r_stage[2].start(r_stage[1].result())
    red[...] = w_stage[2].result() * (1.0 / rows_total)
    fwd.finish()
    bwd.finish()
    meta_stage.close()
    for stage in w_stage + r_stage[:2]:
        stage.close()
    store_gz.wait()
    store_gx.wait()
    red_rates[...] = r_stage[2].result() * (1.0 / rows_total)
    r_stage[2].close()


def hand_over(nb, gx, gz, gb, gc, red, red_rates, gx_out, gz_out, gb_out, gc_out, loss, rate, skip, gain, stage, sems):
    rows = gx.shape[0] // PIECES
    moves = []
    for i, (src, dst) in enumerate(((gx, gx_out), (gz, gz_out))):
        for j in range(PIECES):
            cut, n = pl.ds(j * rows, rows), i * PIECES + j
            moves.append((
                pltpu.make_async_copy(src.at[cut], stage.at[i, cut], sems.at[0, n]),
                pltpu.make_async_copy(stage.at[i, cut], dst.at[cut], sems.at[1, n]),
            ))
    for fetch, _ in moves:
        fetch.start()
    gb_out[...] = gb[...]
    gc_out[...] = gc[...]
    for b in range(nb):
        gain[:, b * LANES : (b + 1) * LANES] = red[b : b + 1, :]
    tail = jnp.sum(red[nb:, :], axis=0, keepdims=True)
    loss[...] = tail[:, LANES - 1 :]
    skip[...] = tail[:, : 2 * nb]
    rate[...] = jnp.sum(red_rates[...], axis=0, keepdims=True)[:, : 2 * nb]
    for fetch, store in moves:
        fetch.wait()
        store.start()
    for _, store in moves:
        store.wait()


def shards(mesh, inputs, gates, keys_b, reads_c, step_codes, seg_starts, targets, log_rates, skips, gains):
    tok, width = inputs.shape[1:]
    nb = width // LANES
    seq, dpn = mesh.shape["seq"], mesh.shape["dp"]
    zr = min(Z_RING, seq)
    xr = seq // zr
    vmem, smem = pl.BlockSpec(memory_space=pltpu.VMEM), pl.BlockSpec(memory_space=pltpu.SMEM)
    hbm = pl.BlockSpec(memory_space=pltpu.HBM)
    rows = nb + 8
    state = pltpu.VMEM((nb, tok, LANES), F32)
    dma = pltpu.SemaphoreType.DMA
    counts = (zr, xr, dpn)
    of = jax.ShapeDtypeStruct
    wide, small = of((tok, width), BF16), of(keys_b.shape[1:], BF16)
    flat, half = pltpu.VMEM((tok, width), F32), pltpu.VMEM((tok, width), BF16)
    results = pl.pallas_call(
        functools.partial(kernel, xr, zr, dpn, nb, float(tok * seq * dpn)),
        out_shape=(wide, wide, small, small, of((rows, LANES), F32), of((8, LANES), F32)),
        in_specs=[smem] * 2 + [hbm] * 3 + [vmem] * 5,
        out_specs=(hbm,) * 2 + (vmem,) * 4,
        scratch_shapes=[half] * 5
        + [state] * 8
        + [
            flat,
            flat,
            flat,
            pltpu.VMEM((nb, tok, LANES), BF16),
            half,
            pltpu.VMEM((6, tok, LANES), F32),
            pltpu.VMEM((4, tok, tok), F32),
            pltpu.VMEM((7, tok, LANES), F32),
            pltpu.VMEM((nb, 8, LANES), F32),
            pltpu.VMEM((nb, 8, LANES), F32),
            pltpu.VMEM((nb, 8, LANES), F32),
            pltpu.VMEM((LANES, tok), BF16),
            pltpu.VMEM((LANES, tok), BF16),
            pltpu.VMEM((11, 8, LANES), F32),
            pltpu.VMEM((zr, 8, LANES), F32),
            [pltpu.VMEM((n, rows, LANES), F32) for n in counts],
            [pltpu.VMEM((n, 8, LANES), F32) for n in counts],
        ]
        + [[dma((nb * SPLIT,))] * 6, dma((12,)), dma((5,))]
        + [[[dma((n,)), dma((n,))] for n in counts] for _ in range(2)]
        + [[dma((zr,)), dma((zr,))]],
        compiler_params=pltpu.CompilerParams(
            collective_id=0, has_side_effects=True, vmem_limit_bytes=56 * 1024 * 1024
        ),
        name="mixer",
    )(
        log_rates, skips, inputs[0], gates[0], targets[0], keys_b[0], reads_c[0],
        step_codes, seg_starts, gains.reshape(1, width),
    )
    line = of((1, 2 * nb), F32)
    gx, gz, gb, gc, loss, rate, skip, gain = pl.pallas_call(
        functools.partial(hand_over, nb),
        out_shape=(wide, wide, small, small, of((1, 1), F32), line, line, of((1, width), F32)),
        in_specs=[hbm] * 2 + [vmem] * 4,
        out_specs=(hbm,) * 2 + (vmem,) * 6,
        scratch_shapes=[pltpu.VMEM((2, tok, width), BF16), dma((2, 2 * PIECES))],
        name="hand_over",
    )(*results)
    return (
        loss[0, 0], gx[None], gz[None], gb[None], gc[None], rate[0], skip[0], gain[0],
    )


def solution(mesh):
    wide, line = P("dp", "seq", None), P("dp", "seq")
    return jax.shard_map(
        functools.partial(shards, mesh),
        mesh=mesh,
        in_specs=(wide, wide, wide, wide, line, line, wide, P(), P(), P()),
        out_specs=(P(), wide, wide, wide, wide, P(), P(), P()),
        check_vma=False,
    )
```
